128 devices in a mesh: prow: 8 (over x, core), pcol: 16 (over y, z).
Axes of the slice: x: 4, y: 4, z: 4, core: 2. Of those that a mesh axis runs over, the one named last changes fastest.
Arguments:
- front: float32 [59, 8, 128, 1, 16, 128], P(None, 'prow', None, None, 'pcol'), may hold values from -66 to 396
- child: float32 [2, 8, 8, 128, 16, 128], P(None, None, 'prow', None, 'pcol'), may hold values from -6 to 6
- row_map: int32 [2, 64], replicated, may hold values from 0 to 471, as said below
- col_map: int32 [2, 16], replicated, may hold values from 0 to 15, as said below
Outputs:
- factor: float32 [59, 8, 128, 1, 16, 128], P(None, 'prow', None, None, 'pcol')
The draws below stay inside these ranges and needn't reach their ends.
Inputs may be any that keep to these rules, and one draw needn't show every extreme that they name: Within one child all entries differ. For each child c and each index p of prow, the entries row_map[c, l * 8 + p] for l = 0 .. 7 have different remainders modulo 8. `col_map`: within one child all entries differ.
All inputs are finite; a program needn't handle non-finite values.
Results may differ from the reference program's by a relative error of at most 0.0001.
Values sent between devices are 32-bit elements; how exact they have to be, the bound alone decides.
No kernel may reach another device: no remote copies, remote signals or barrier semaphores. Data moves between devices by JAX's collectives and lax.ppermute only.
A program may use at most 128 MiB of HBM per device.

```python
import jax
import jax.numpy as jnp
from jax import lax

BS = 128
NF = 60416
CBL = 1
RBL = 59
KRL = 8
KR = 64
KC = 16
N_PROW = 8
N_PCOL = 16


def draw_front(key, part):
    key = jax.random.fold_in(key, 11)
    noise_key, left_key, down_key = jax.random.split(key, 3)
    shape = (RBL, N_PROW, BS, CBL, N_PCOL, BS)
    values = jax.random.truncated_normal(noise_key, -6.0, 6.0, shape, jnp.float32)
    rows = (lax.broadcasted_iota(jnp.int32, shape, 0) * N_PROW + lax.broadcasted_iota(jnp.int32, shape, 1)) * BS + lax.broadcasted_iota(jnp.int32, shape, 2)
    cols = (lax.broadcasted_iota(jnp.int32, shape, 3) * N_PCOL + lax.broadcasted_iota(jnp.int32, shape, 4)) * BS + lax.broadcasted_iota(jnp.int32, shape, 5)
    leading = 4 * BS
    left_index = jnp.arange(leading + 1)
    left_weight = jax.random.uniform(left_key, (leading + 1,), jnp.float32, 20.0, 60.0)
    left_weight = jnp.where((left_index % 16 == 0) | (left_index >= leading), 0.0, left_weight)
    down_index = jnp.arange(leading + 16)
    down_weight = jax.random.uniform(down_key, (leading + 16,), jnp.float32, 20.0, 60.0)
    down_weight = jnp.where((down_index < 16) | (down_index >= leading), 0.0, down_weight)
    centre = 150.0 + left_weight[:leading] + left_weight[1:leading + 1] + down_weight[:leading] + down_weight[16:leading + 16]
    safe_row = jnp.minimum(rows, leading - 1)
    inside = (rows < leading) & (cols < leading)
    coupling = jnp.where(rows == cols, centre[safe_row], 0.0)
    coupling = coupling - jnp.where(cols == rows - 1, left_weight[safe_row], 0.0)
    coupling = coupling - jnp.where(cols == rows - 16, down_weight[safe_row], 0.0)
    return values + jnp.where(inside, coupling, 0.0)


def shuffle_rows(subkey):
    return jax.random.permutation(subkey, RBL)


def draw_row_map(key, part):
    key = jax.random.fold_in(key, 23)
    subkeys = jax.random.split(key, 2 * N_PROW + 1)
    orders = jax.vmap(shuffle_rows)(subkeys[:-1]).reshape(2, N_PROW, RBL)[:, :, :N_PROW]
    shifts = jax.random.randint(subkeys[-1], (2,), 0, N_PROW)
    local = jnp.arange(N_PROW)[None, :, None]
    source = jnp.arange(N_PROW)[None, None, :]
    target = (source + local + shifts[:, None, None]) % N_PROW
    chosen = orders[jnp.arange(2)[:, None, None], target, local]
    return (chosen * N_PROW + target).reshape(2, N_PROW * N_PROW).astype(jnp.int32)


def shuffle_cols(subkey):
    return jax.random.permutation(subkey, CBL * N_PCOL)[:N_PCOL]


def draw_col_map(key, part):
    key = jax.random.fold_in(key, 37)
    subkeys = jax.random.split(key, 2)
    return jax.vmap(shuffle_cols)(subkeys).astype(jnp.int32)


def steps_of(key, extent, cuts, smallest, largest):
    def one(dim, parts):
        heights = jax.random.uniform(jax.random.fold_in(jax.random.fold_in(key, 6), dim), (parts,), jnp.float32, smallest / len(cuts), largest / len(cuts))
        return jnp.repeat(jnp.exp(heights), extent[dim] // parts).reshape((-1,) + (1,) * (len(extent) - dim - 1))

    gain = one(*cuts[0])
    for cut in cuts[1:]:
        gain = gain * one(*cut)
    return gain


def bell_draw(key, shape, deviation, most, pieces=(), held_as=jnp.bfloat16):
    result = deviation * jax.random.normal(key, shape, jnp.float32)
    if pieces:
        result = result * steps_of(key, shape, pieces, -0.22, 0.18)
    return jnp.clip(result, -most, most).astype(held_as)


def setup_inputs(seed: int = 0) -> dict:
    seeds = jax.random.split(jax.random.key(seed), 5)
    front = draw_front(jax.random.fold_in(seeds[4], 71), 0)
    child = bell_draw(seeds[1], (2, KRL, N_PROW, BS, N_PCOL, BS), 1.0, 6.0, ((2, 8), (4, 16)), jnp.float32)
    row_map = draw_row_map(jax.random.fold_in(seeds[4], 71), 0)
    col_map = draw_col_map(jax.random.fold_in(seeds[4], 71), 0)
    return dict(front=front, child=child, row_map=row_map, col_map=col_map)


HIGHEST_PRECISION = lax.Precision.HIGHEST

def reference(front, child, row_map, col_map):
    col_total = CBL * N_PCOL * BS
    blocks = front.reshape(NF // BS, BS, CBL * N_PCOL, BS)
    for member in range(2):
        piece = child[member].reshape(KR, BS, KC, BS).transpose(0, 2, 1, 3)
        blocks = blocks.at[row_map[member][:, None], :, col_map[member][None, :], :].add(piece)
    matrix = blocks.reshape(NF, col_total)
    for segment in range(2):
        start_col = 2 * segment * BS
        stop_col = start_col + 2 * BS
        diag = matrix[start_col:stop_col, start_col:stop_col]
        sym = jnp.tril(diag) + jnp.tril(diag, -1).T
        lower = jnp.linalg.cholesky(sym)
        inverse = lax.linalg.triangular_solve(lower, jnp.eye(2 * BS, dtype=jnp.float32), left_side=True, lower=True)
        factor = jnp.dot(matrix[:, start_col:stop_col], inverse.T, precision=HIGHEST_PRECISION)
        factor = factor.at[start_col:stop_col].set(lower)
        matrix = matrix.at[:, start_col:stop_col].set(factor)
        change = jnp.dot(factor, factor[stop_col:col_total].T, precision=HIGHEST_PRECISION)
        matrix = matrix.at[:, stop_col:].add(-change)
    rows = jnp.arange(NF)[:, None]
    cols = jnp.arange(col_total)[None, :]
    keep = rows >= jnp.minimum(cols, 4 * BS)
    return jnp.where(keep, matrix, 0.0).reshape(front.shape)
```

```python
import functools

import jax
import jax.numpy as jnp
from jax import lax
from jax.experimental import pallas as pl
from jax.experimental.pallas import tpu as pltpu
from jax.sharding import PartitionSpec as P

BS = 128
TOP = 4
PROWS = 8
PCOLS = 16
SUB = 32
GROUP = 4
BOTH = ("prow", "pcol")
NN = (((1,), (0,)), ((), ()))
NT = (((1,), (1,)), ((), ()))
TN = (((0,), (0,)), ((), ()))
VMEM_LIMIT = 48 << 20


def vmem():
    return pl.BlockSpec(memory_space=pltpu.VMEM)


def smem():
    return pl.BlockSpec(memory_space=pltpu.SMEM)


def params():
    return pltpu.CompilerParams(vmem_limit_bytes=VMEM_LIMIT)


def exact_dot(a, b, dims=NN):
    return lax.dot_general(
        a, b, dims, precision=lax.Precision.HIGHEST, preferred_element_type=jnp.float32
    )


def route_kernel(col_ref, table_ref, got_ref, onward_ref, top_ref, inverse, pack):
    for c in range(2):
        for q in range(PCOLS):
            inverse[c, col_ref[c, q]] = q
    out_id = lax.broadcasted_iota(jnp.int32, (64, 64), 0)
    in_id = lax.broadcasted_iota(jnp.int32, (64, 64), 1)
    wanted = lax.broadcasted_iota(jnp.int32, (16, 64), 0)
    sums = [
        jnp.concatenate([got_ref[:, k, 16 + s, :] for s in range(2)], axis=0)
        for k in range(TOP)
    ]
    for c in range(2):
        table = table_ref[c : c + 1, :]
        move = (out_id % 8 == in_id // 8) & (out_id // 8 == jnp.broadcast_to(table, (64, 64)) % 8)
        move = move.astype(jnp.float32)
        pick = (wanted == jnp.broadcast_to(table, (16, 64))).astype(jnp.float32)
        for q in range(PCOLS):
            source = inverse[c, q]
            rows = got_ref[:, source, 8 * c : 8 * c + 8, :].reshape(64, BS)
            onward_ref[:, q, 8 * c : 8 * c + 8, :] = exact_dot(move, rows).reshape(8, 8, BS)
            if q < TOP:
                sums[q] = sums[q] + exact_dot(pick, rows)
    pack[...] = jnp.zeros_like(pack)
    place = 0
    for t in range(TOP):
        for k in range(t + 1):
            pack[place : place + 1, :] = sums[k][t : t + 1, :]
            place += 1
    for q in range(PCOLS):
        for k in range(TOP):
            pack[place + k : place + k + 1, :] = sums[k][q : q + 1, :]
        top_ref[:, q] = jnp.broadcast_to(pack[...][None], (PROWS, 16, BS))


def route(col_map, table, got):
    return pl.pallas_call(
        route_kernel,
        out_shape=(
            jax.ShapeDtypeStruct((PROWS, PCOLS, 16, BS), jnp.float32),
            jax.ShapeDtypeStruct((PROWS, PCOLS, 16, BS), jnp.float32),
        ),
        in_specs=[smem(), vmem(), vmem()],
        out_specs=[vmem(), vmem()],
        scratch_shapes=[pltpu.SMEM((2, PCOLS), jnp.int32), pltpu.VMEM((16, BS), jnp.float32)],
        compiler_params=params(),
        name="route",
    )(col_map, table, got)


def factor_block(tab, up, width):
    for k0 in range(0, BS, width):
        rows = [jnp.broadcast_to(tab[k0 + i : k0 + i + 1, :], (8, 2 * BS)) for i in range(width)]
        a = [
            [jnp.broadcast_to(rows[i][:, k0 + j : k0 + j + 1], (8, BS)) for j in range(i + 1)]
            for i in range(width)
        ]
        scale = [None] * width
        for j in range(width):
            scale[j] = lax.rsqrt(a[j][j])
            for i in range(j + 1, width):
                a[i][j] = a[i][j] * scale[j]
            for i in range(j + 1, width):
                for m in range(j + 1, i + 1):
                    a[i][m] = a[i][m] - a[i][j] * a[m][j]
        done = []
        for i in range(width):
            halves = []
            for h in range(2):
                u = rows[i][:, h * BS : (h + 1) * BS]
                for j in range(i):
                    u = u - a[i][j] * done[j][h]
                halves.append(u * scale[i])
            done.append(halves)
            up[k0 + i : k0 + i + 1, 0:BS] = halves[0][0:1]
            up[k0 + i : k0 + i + 1, BS:] = halves[1][0:1]
        after = k0 + width
        if after < BS:
            panel = up[k0:after, :]
            tab[after:, :] = tab[after:, :] - exact_dot(panel[:, :BS], panel, TN)[after:, :]


def cholesky_kernel(width, place_ref, got_ref, weight_ref, top_ref, work, low, tab, up, inverses):
    row = lax.broadcasted_iota(jnp.int32, (BS, BS), 0)
    col = lax.broadcasted_iota(jnp.int32, (BS, BS), 1)
    eye = (row == col).astype(jnp.float32)
    place = 0
    for t in range(TOP):
        for k in range(t + 1):
            work[t * BS : (t + 1) * BS, k * BS : (k + 1) * BS] = got_ref[:, place, :]
            place += 1
    for k in range(TOP):
        work[TOP * BS :, k * BS : (k + 1) * BS] = got_ref[:, place + k, :]
    low[...] = jnp.zeros_like(low)
    for k in range(TOP):
        lo, hi = k * BS, (k + 1) * BS
        block = work[lo:hi, lo:hi]
        tab[:, :BS] = jnp.where(row >= col, block, block.T)
        tab[:, BS:] = eye
        factor_block(tab, up, width)
        low[lo:hi, lo:hi] = jnp.where(row >= col, up[:, :BS].T, 0.0)
        inverse = up[:, BS:]
        inverses[lo:hi, :] = inverse
        below = exact_dot(work[hi:, lo:hi], inverse, NT)
        work[hi:, lo:hi] = below
        if k + 1 < TOP:
            count = (TOP - 1 - k) * BS
            low[hi:, lo:hi] = below[:count]
            work[hi:, hi:] = work[hi:, hi:] - exact_dot(below, below[:count], NT)
    my_row = place_ref[0]
    my_col = place_ref[1]
    for k in reversed(range(TOP)):
        lo, hi = k * BS, (k + 1) * BS
        solved = work[TOP * BS :, lo:hi].T
        rhs = jnp.where(my_col >= TOP, solved, jnp.where(my_col == k, -eye, 0.0))
        if k + 1 < TOP:
            rhs = rhs - exact_dot(work[hi : TOP * BS, lo:hi], weight_ref[hi:, :], TN)
        weight_ref[lo:hi, :] = exact_dot(inverses[lo:hi, :], rhs, TN)
    r0 = pl.multiple_of(jnp.minimum(my_row, TOP - 1) * BS, BS)
    c0 = pl.multiple_of(jnp.minimum(my_col, TOP - 1) * BS, BS)
    top_ref[...] = jnp.where(my_col < TOP, low[pl.ds(r0, BS), pl.ds(c0, BS)], 0.0)


def cholesky(place, got):
    return pl.pallas_call(
        functools.partial(cholesky_kernel, 16),
        out_shape=(
            jax.ShapeDtypeStruct((TOP * BS, BS), jnp.float32),
            jax.ShapeDtypeStruct((BS, BS), jnp.float32),
        ),
        in_specs=[smem(), vmem()],
        out_specs=[vmem(), vmem()],
        scratch_shapes=[
            pltpu.VMEM(((TOP + 1) * BS, TOP * BS), jnp.float32),
            pltpu.VMEM((TOP * BS, TOP * BS), jnp.float32),
            pltpu.VMEM((BS, 2 * BS), jnp.float32),
            pltpu.VMEM((BS, 2 * BS), jnp.float32),
            pltpu.VMEM((TOP * BS, BS), jnp.float32),
        ],
        compiler_params=params(),
        name="cholesky",
    )(place, got)


def assemble_kernel(slot_ref, f0, f1, f2, f3, c0, c1, c2, c3, out_ref):
    out_ref[...] = f0[...] + f1[...] + f2[...] + f3[...]
    for i in range(16):
        slot = slot_ref[i]
        out_ref[slot] = out_ref[slot] + (c0[i] + c1[i] + c2[i] + c3[i])


def assemble(slots, front_parts, child_parts):
    return pl.pallas_call(
        assemble_kernel,
        out_shape=jax.ShapeDtypeStruct(front_parts[0].shape, jnp.float32),
        in_specs=[smem()] + [vmem()] * 8,
        out_specs=vmem(),
        compiler_params=params(),
        name="assemble",
    )(slots, *front_parts, *child_parts)


def update_kernel(place_ref, which_ref, weight_ref, top_ref, child_ref, panel_ref, front_ref, out_ref, high, wide):
    step = pl.program_id(0)

    @pl.when(step == 0)
    def _():
        weight = weight_ref[...]
        big = weight.astype(jnp.bfloat16)
        small = (weight - big.astype(jnp.float32)).astype(jnp.bfloat16)
        high[...] = big
        wide[...] = jnp.concatenate([big, small], axis=1)

    rows = GROUP * BS
    parts = []
    for z in range(TOP):
        piece = jnp.stack([panel_ref[4 * y + z] for y in range(4)], axis=1)
        parts.append(piece.reshape(rows, BS))
    panel = jnp.concatenate(parts, axis=1)
    big = panel.astype(jnp.bfloat16)
    small = (panel - big.astype(jnp.float32)).astype(jnp.bfloat16)
    first = lax.dot_general(big, wide[...], NN, preferred_element_type=jnp.float32)
    second = lax.dot_general(small, high[...], NN, preferred_element_type=jnp.float32)
    change = first[:, :BS] + (first[:, BS:] + second)
    base = jnp.where(place_ref[1] >= TOP, front_ref[...], 0.0)
    out_ref[...] = base - change.reshape(GROUP, BS, BS)
    for i in range(GROUP):
        for c in range(2):
            source = which_ref[c, step * GROUP + i]

            @pl.when((source >= 0) & (place_ref[1] >= TOP))
            def _():
                out_ref[i] = out_ref[i] + child_ref[jnp.maximum(source, 0)]

    @pl.when((step == 0) & (place_ref[0] < TOP))
    def _():
        out_ref[0] = top_ref[...]


def update(place, which, weight, top, child, panel, front):
    count = front.shape[0]
    return pl.pallas_call(
        update_kernel,
        out_shape=jax.ShapeDtypeStruct(front.shape, jnp.float32),
        grid=(pl.cdiv(count, GROUP),),
        in_specs=[
            smem(),
            smem(),
            vmem(),
            vmem(),
            vmem(),
            pl.BlockSpec((PCOLS, GROUP, SUB, BS), lambda i: (0, i, 0, 0)),
            pl.BlockSpec((GROUP, BS, BS), lambda i: (i, 0, 0)),
        ],
        out_specs=pl.BlockSpec((GROUP, BS, BS), lambda i: (i, 0, 0)),
        scratch_shapes=[
            pltpu.VMEM((TOP * BS, BS), jnp.bfloat16),
            pltpu.VMEM((TOP * BS, 2 * BS), jnp.bfloat16),
        ],
        compiler_params=params(),
        name="update",
    )(place, which, weight, top, child, panel, front)


def scatter_rows(blocks):
    lane = lax.axis_index("pcol")
    parts = [jnp.where(lane < TOP, blocks[:, :SUB], 0.0)]
    for y in range(1, 4):
        pairs = [(k, 4 * y + k) for k in range(TOP)]
        parts.append(lax.ppermute(blocks[:, y * SUB : (y + 1) * SUB], "pcol", pairs))
    return parts


def on_device(front, child, row_map, col_map):
    count = front.shape[0]
    row_here = lax.axis_index("prow")
    col_here = lax.axis_index("pcol")
    place = jnp.stack([row_here, col_here]).astype(jnp.int32)
    blocks = front.reshape(count, BS, BS)
    pieces = child.reshape(16, BS, BS)
    by_source = row_map.reshape(2, 8, PROWS).transpose(0, 2, 1)
    table = by_source.reshape(2, 64)
    mine = by_source % PROWS == row_here
    slots = jnp.sum(jnp.where(mine, by_source // PROWS, 0), axis=2)
    padded = pl.cdiv(count, GROUP) * GROUP
    hit = slots[:, :, None] == jnp.arange(padded)[None, None, :]
    which = jnp.max(jnp.where(hit, jnp.arange(16).reshape(2, 8, 1), -1), axis=1)
    front_parts = scatter_rows(blocks)
    first = jnp.concatenate([pieces, blocks[:2], jnp.zeros((6, BS, BS), jnp.float32)])
    got = lax.all_to_all(first.transpose(1, 0, 2), BOTH, 0, 0, tiled=True)
    onward, tops = route(col_map, table, got.reshape(PROWS, PCOLS, 24, BS))
    arrived = lax.all_to_all(onward.reshape(BS, 16, BS), BOTH, 0, 0, tiled=True)
    arrived = arrived.transpose(1, 0, 2)
    child_parts = scatter_rows(arrived)
    chunk = assemble(slots.reshape(16), front_parts, child_parts)
    panel = lax.all_gather(chunk, "pcol")
    known = lax.all_to_all(tops.reshape(BS, 16, BS), BOTH, 0, 0, tiled=True)
    weight, top = cholesky(place, known)
    result = update(place, which, weight, top, arrived, panel, blocks)
    return result.reshape(front.shape)


def solution(mesh):
    return jax.shard_map(
        on_device,
        mesh=mesh,
        in_specs=(
            P(None, "prow", None, None, "pcol", None),
            P(None, None, "prow", None, "pcol", None),
            P(),
            P(),
        ),
        out_specs=P(None, "prow", None, None, "pcol", None),
        check_vma=False,
    )
```

```python
import functools

import jax
import jax.numpy as jnp
from jax import lax
from jax.experimental import pallas as pl
from jax.experimental.pallas import tpu as pltpu
from jax.sharding import PartitionSpec as P

BS = 128
TOP = 4
PROWS = 8
PCOLS = 16
SUB = 32
GROUP = 10
PART = 30
WIDE = 32
BOTH = ("prow", "pcol")
NN = (((1,), (0,)), ((), ()))
NT = (((1,), (1,)), ((), ()))
TN = (((0,), (0,)), ((), ()))
VMEM_LIMIT = 48 << 20


def vmem():
    return pl.BlockSpec(memory_space=pltpu.VMEM)


def smem():
    return pl.BlockSpec(memory_space=pltpu.SMEM)


def params():
    return pltpu.CompilerParams(vmem_limit_bytes=VMEM_LIMIT)


def exact_dot(a, b, dims=NN):
    return lax.dot_general(
        a, b, dims, precision=lax.Precision.HIGHEST, preferred_element_type=jnp.float32
    )


def route_kernel(col_ref, table_ref, got_ref, panel_ref, mixed_ref, inverse, pack):
    for c in range(2):
        for q in range(PCOLS):
            inverse[c, col_ref[c, q]] = q
    out_id = lax.broadcasted_iota(jnp.int32, (64, 64), 0)
    in_id = lax.broadcasted_iota(jnp.int32, (64, 64), 1)
    wanted = lax.broadcasted_iota(jnp.int32, (16, 64), 0)
    sums = [
        jnp.concatenate([got_ref[:, k, 16 + s, :] for s in range(2)], axis=0)
        for k in range(TOP)
    ]
    for c in range(2):
        table = table_ref[c : c + 1, :]
        move = (out_id % 8 == in_id // 8) & (out_id // 8 == jnp.broadcast_to(table, (64, 64)) % 8)
        move = move.astype(jnp.float32)
        pick = (wanted == jnp.broadcast_to(table, (16, 64))).astype(jnp.float32)
        for q in range(PCOLS):
            source = inverse[c, q]
            rows = got_ref[:, source, 8 * c : 8 * c + 8, :].reshape(64, BS)
            moved = exact_dot(move, rows).reshape(8, 8, BS)
            if q < TOP:
                sums[q] = sums[q] + exact_dot(pick, rows)
                panel_ref[q, :, 8 * c : 8 * c + 8, :] = moved
                mixed_ref[:, q, 16 + 8 * c : 24 + 8 * c, :] = jnp.zeros_like(moved)
            else:
                mixed_ref[:, q, 16 + 8 * c : 24 + 8 * c, :] = moved
    pack[...] = jnp.zeros_like(pack)
    place = 0
    for t in range(TOP):
        for k in range(t + 1):
            pack[place : place + 1, :] = sums[k][t : t + 1, :]
            place += 1
    for q in range(PCOLS):
        for k in range(TOP):
            pack[place + k : place + k + 1, :] = sums[k][q : q + 1, :]
        mixed_ref[:, q, :16] = jnp.broadcast_to(pack[...][None], (PROWS, 16, BS))


def route(col_map, table, got):
    return pl.pallas_call(
        route_kernel,
        out_shape=(
            jax.ShapeDtypeStruct((TOP, PROWS, 16, BS), jnp.float32),
            jax.ShapeDtypeStruct((PROWS, PCOLS, WIDE, BS), jnp.float32),
        ),
        in_specs=[smem(), vmem(), vmem()],
        out_specs=[vmem(), vmem()],
        scratch_shapes=[pltpu.SMEM((2, PCOLS), jnp.int32), pltpu.VMEM((16, BS), jnp.float32)],
        compiler_params=params(),
        name="route",
    )(col_map, table, got)


def factor_block(tab, up, width):
    for k0 in range(0, BS, width):
        rows = [jnp.broadcast_to(tab[k0 + i : k0 + i + 1, :], (8, 2 * BS)) for i in range(width)]
        a = [
            [jnp.broadcast_to(rows[i][:, k0 + j : k0 + j + 1], (8, BS)) for j in range(i + 1)]
            for i in range(width)
        ]
        scale = [None] * width
        for j in range(width):
            scale[j] = lax.rsqrt(a[j][j])
            for i in range(j + 1, width):
                a[i][j] = a[i][j] * scale[j]
            for i in range(j + 1, width):
                for m in range(j + 1, i + 1):
                    a[i][m] = a[i][m] - a[i][j] * a[m][j]
        done = []
        for i in range(width):
            halves = []
            for h in range(2):
                u = rows[i][:, h * BS : (h + 1) * BS]
                for j in range(i):
                    u = u - a[i][j] * done[j][h]
                halves.append(u * scale[i])
            done.append(halves)
            up[k0 + i : k0 + i + 1, 0:BS] = halves[0][0:1]
            up[k0 + i : k0 + i + 1, BS:] = halves[1][0:1]
        after = k0 + width
        if after < BS:
            panel = up[k0:after, :]
            tab[after:, :] = tab[after:, :] - exact_dot(panel[:, :BS], panel, TN)[after:, :]


def load(got_ref, place, work, row, col):
    for yz in range(PCOLS):
        rows = got_ref[pl.ds(yz * WIDE + place, PROWS, stride=PCOLS * WIDE), :]
        work[row + 8 * yz : row + 8 * yz + 8, col : col + BS] = rows


def cholesky_steps(steps, width, work, diagonal, inverses, tab, up):
    row = lax.broadcasted_iota(jnp.int32, (BS, BS), 0)
    col = lax.broadcasted_iota(jnp.int32, (BS, BS), 1)
    for k in steps:
        lo, hi = k * BS, (k + 1) * BS
        block = work[lo:hi, lo:hi]
        tab[:, :BS] = jnp.where(row >= col, block, block.T)
        tab[:, BS:] = (row == col).astype(jnp.float32)
        factor_block(tab, up, width)
        diagonal[lo:hi, :] = jnp.where(row >= col, up[:, :BS].T, 0.0)
        inverse = up[:, BS:]
        inverses[lo:hi, :] = inverse
        below = exact_dot(work[hi:, lo:hi], inverse, NT)
        work[hi:, lo:hi] = below
        if k + 1 < TOP:
            work[hi:, hi:] = work[hi:, hi:] - exact_dot(below, below[: (TOP - 1 - k) * BS], NT)


def first_kernel(width, steps, got_ref, work, diagonal, inverses, tab, up):
    place = 0
    for t in range(TOP):
        for k in range(t + 1):
            load(got_ref, place, work, t * BS, k * BS)
            place += 1
        for k in range(t + 1, TOP):
            work[t * BS : (t + 1) * BS, k * BS : (k + 1) * BS] = jnp.zeros((BS, BS), jnp.float32)
    for k in range(TOP):
        load(got_ref, place + k, work, TOP * BS, k * BS)
    diagonal[...] = jnp.zeros_like(diagonal)
    inverses[...] = jnp.zeros_like(inverses)
    cholesky_steps(steps, width, work, diagonal, inverses, tab, up)


def last_kernel(width, steps, place_ref, work, diagonal, inverses, weight_ref, top_ref, tab, up):
    cholesky_steps(steps, width, work, diagonal, inverses, tab, up)
    row = lax.broadcasted_iota(jnp.int32, (BS, BS), 0)
    col = lax.broadcasted_iota(jnp.int32, (BS, BS), 1)
    eye = (row == col).astype(jnp.float32)
    my_row = place_ref[0]
    my_col = place_ref[1]
    for k in reversed(range(TOP)):
        lo, hi = k * BS, (k + 1) * BS
        solved = work[TOP * BS :, lo:hi].T
        rhs = jnp.where(my_col >= TOP, solved, jnp.where(my_col == k, -eye, 0.0))
        if k + 1 < TOP:
            rhs = rhs - exact_dot(work[hi : TOP * BS, lo:hi], weight_ref[hi:, :], TN)
        weight_ref[lo:hi, :] = exact_dot(inverses[lo:hi, :], rhs, TN)
    r0 = pl.multiple_of(jnp.minimum(my_row, TOP - 1) * BS, BS)
    c0 = pl.multiple_of(jnp.minimum(my_col, TOP - 1) * BS, BS)
    found = jnp.where(my_row > my_col, work[pl.ds(r0, BS), pl.ds(c0, BS)], 0.0)
    top_ref[...] = jnp.where(my_row == my_col, diagonal[pl.ds(r0, BS), :], found)


STATE = (((TOP + 1) * BS, TOP * BS), (TOP * BS, BS), (TOP * BS, BS))


def factor_scratch():
    return [pltpu.VMEM((BS, 2 * BS), jnp.float32)] * 2


def cholesky_first(got):
    return pl.pallas_call(
        functools.partial(first_kernel, 16, (0, 1)),
        out_shape=[jax.ShapeDtypeStruct(s, jnp.float32) for s in STATE],
        in_specs=[vmem()],
        out_specs=[vmem()] * 3,
        scratch_shapes=factor_scratch(),
        compiler_params=params(),
        cost_estimate=pl.CostEstimate(flops=15 * 10**9, bytes_accessed=4 << 20, transcendentals=0),
        name="cholesky_first",
    )(got.reshape(BS * WIDE, BS))


def cholesky_last(place, state):
    def kernel(place_ref, w_in, d_in, i_in, weight_ref, top_ref, work, diagonal, inverses, tab, up):
        work[...] = w_in[...]
        diagonal[...] = d_in[...]
        inverses[...] = i_in[...]
        last_kernel(16, (2, 3), place_ref, work, diagonal, inverses, weight_ref, top_ref, tab, up)

    return pl.pallas_call(
        kernel,
        out_shape=(
            jax.ShapeDtypeStruct((TOP * BS, BS), jnp.float32),
            jax.ShapeDtypeStruct((BS, BS), jnp.float32),
        ),
        in_specs=[smem()] + [vmem()] * 3,
        out_specs=[vmem(), vmem()],
        scratch_shapes=[pltpu.VMEM(s, jnp.float32) for s in STATE] + factor_scratch(),
        compiler_params=params(),
        cost_estimate=pl.CostEstimate(flops=15 * 10**9, bytes_accessed=4 << 20, transcendentals=0),
        name="cholesky_last",
    )(place, *state)


def assemble_kernel(place_ref, slot_ref, f0, f1, f3, low, high, child_ref, out_ref):
    half = low.shape[0]
    first = jnp.where(place_ref[1] < TOP, f0[...], f1[...] + f3[...])
    out_ref[:half] = first[:half] + low[...]
    out_ref[half:] = first[half:] + high[...]
    for i in range(16):
        slot = slot_ref[i]
        out_ref[slot] = out_ref[slot] + child_ref[:, i, :]


def assemble(place, slots, *parts):
    return pl.pallas_call(
        assemble_kernel,
        out_shape=jax.ShapeDtypeStruct(parts[0].shape, jnp.float32),
        in_specs=[smem(), smem()] + [vmem()] * 6,
        out_specs=vmem(),
        compiler_params=params(),
        name="assemble",
    )(place, slots, *parts)


def update_kernel(steps, place_ref, which_ref, weight_ref, top_ref, child_ref, *refs):
    first, second, (front_ref, out_ref, high, wide) = refs[:8], refs[8:16], refs[16:]
    step = pl.program_id(0)
    mine = place_ref[1] >= TOP
    my_y = place_ref[1] // 4
    my_z = place_ref[1] % 4

    @pl.when(step == 0)
    def _():
        for dz in range(4):
            start = pl.multiple_of((my_z + 4 - dz) % 4 * BS, BS)
            weight = weight_ref[pl.ds(start, BS), :]
            big = weight.astype(jnp.bfloat16)
            high[dz * BS : (dz + 1) * BS, :] = big
            wide[dz * BS : (dz + 1) * BS, :BS] = big
            wide[dz * BS : (dz + 1) * BS, BS:] = (weight - big.astype(jnp.float32)).astype(jnp.bfloat16)

    def finish(read):
        for dy in range(4):
            panel = jnp.concatenate([read(dy, dz).reshape(GROUP * SUB, BS) for dz in range(4)], axis=1)
            big = panel.astype(jnp.bfloat16)
            small = (panel - big.astype(jnp.float32)).astype(jnp.bfloat16)
            one = lax.dot_general(big, wide[...], NN, preferred_element_type=jnp.float32)
            two = lax.dot_general(small, high[...], NN, preferred_element_type=jnp.float32)
            change = (one[:, :BS] + (one[:, BS:] + two)).reshape(GROUP, SUB, BS)
            rows = pl.ds(pl.multiple_of((my_y + 4 - dy) % 4 * SUB, SUB), SUB)
            out_ref[:, rows, :] = jnp.where(mine, front_ref[:, rows, :], 0.0) - change

    @pl.when(step < steps)
    def _():
        finish(lambda dy, dz: first[2 * dy + dz // 2][dz % 2])

    @pl.when(step >= steps)
    def _():
        finish(lambda dy, dz: second[2 * dz + dy // 2][dy % 2])

    @pl.when(mine)
    def _():
        for i in range(GROUP):
            for c in range(2):
                source = which_ref[c, step * GROUP + i]

                @pl.when(source >= 0)
                def _():
                    out_ref[i] = out_ref[i] + child_ref[jnp.maximum(source, 0)]

    @pl.when((step == 0) & (place_ref[0] < TOP))
    def _():
        out_ref[0] = top_ref[...]


def update(place, which, weight, top, child, first, second, front):
    count = front.shape[0]
    steps = PART // GROUP
    early = lambda i: (0, jnp.minimum(i, steps - 1), 0, 0)
    late = lambda i: (0, jnp.maximum(i - steps, 0), 0, 0)
    specs = [pl.BlockSpec((x.shape[0], GROUP, SUB, BS), early) for x in first]
    specs += [pl.BlockSpec((x.shape[0], GROUP, SUB, BS), late) for x in second]
    return pl.pallas_call(
        functools.partial(update_kernel, steps),
        out_shape=jax.ShapeDtypeStruct(front.shape, jnp.float32),
        grid=(pl.cdiv(count, GROUP),),
        in_specs=[smem(), smem(), vmem(), vmem(), vmem()]
        + specs
        + [pl.BlockSpec((GROUP, BS, BS), lambda i: (i, 0, 0))],
        out_specs=pl.BlockSpec((GROUP, BS, BS), lambda i: (i, 0, 0)),
        scratch_shapes=[
            pltpu.VMEM((TOP * BS, BS), jnp.bfloat16),
            pltpu.VMEM((TOP * BS, 2 * BS), jnp.bfloat16),
        ],
        compiler_params=params(),
        cost_estimate=pl.CostEstimate(flops=10**10, bytes_accessed=24 << 20, transcendentals=0),
        name="update",
    )(place, which, weight, top, child, *first, *second, front)


Y_STEP = 4
Z_STEP = 1


def shift(x, axis, by):
    if axis == Y_STEP:
        pairs = [(4 * y + z, 4 * ((y + by) % 4) + z) for y in range(4) for z in range(4)]
    else:
        pairs = [(4 * y + z, 4 * y + (z + by) % 4) for y in range(4) for z in range(4)]
    return lax.ppermute(x, "pcol", pairs)


SAME_Y = [[p * PCOLS + 4 * y + z for z in range(4) for p in range(PROWS)] for y in range(4)]


def hop(x, origin, target):
    return lax.ppermute(x, "pcol", [(4 * origin + z, 4 * target + z) for z in range(4)])


def on_device(front, child, row_map, col_map):
    count = front.shape[0]
    row_here = lax.axis_index("prow")
    col_here = lax.axis_index("pcol")
    place = jnp.stack([row_here, col_here]).astype(jnp.int32)
    blocks = front.reshape(count, BS, BS)
    pieces = child.reshape(16, BS, BS)
    by_source = row_map.reshape(2, 8, PROWS).transpose(0, 2, 1)
    table = by_source.reshape(2, 64)
    mine = by_source % PROWS == row_here
    slots = jnp.sum(jnp.where(mine, by_source // PROWS, 0), axis=2)
    padded = pl.cdiv(count, GROUP) * GROUP
    hit = slots[:, :, None] == jnp.arange(padded)[None, None, :]
    which = jnp.max(jnp.where(hit, jnp.arange(16).reshape(2, 8, 1), -1), axis=1)
    cuts = [blocks[:, y * SUB : (y + 1) * SUB] for y in range(4)]
    half = count // 2
    relay = [hop(cuts[2][:half], 0, 1), hop(cuts[2][half:], 0, 3)]
    sent = [hop(cuts[1], 0, 1), hop(cuts[3], 0, 3)]
    first = jnp.concatenate([pieces, blocks[:2], jnp.zeros((6, BS, BS), jnp.float32)])
    first = first.reshape(24, PCOLS, PROWS, BS).transpose(2, 1, 0, 3).reshape(BS, 24, BS)
    got = lax.all_to_all(first, BOTH, 0, 0, tiled=True)
    got, relay = lax.optimization_barrier((got, relay))
    sent = sent + [hop(relay[0], 1, 2), hop(relay[1], 3, 2)]
    panel, mixed = route(col_map, table, got.reshape(PROWS, PCOLS, 24, BS))
    panel = lax.all_to_all(
        panel.reshape(4 * PROWS, 16, BS), BOTH, 0, 0, tiled=True, axis_index_groups=SAME_Y
    )
    chunk = assemble(place, slots.reshape(16), cuts[0], *sent, panel)
    chunk, mixed = lax.optimization_barrier((chunk, mixed))
    known = lax.all_to_all(mixed.reshape(BS, WIDE, BS), BOTH, 0, 0, tiled=True)
    half = PART // 2
    rings = (Y_STEP, Z_STEP)
    around, pairs = [], []
    for part, ring in ((chunk[:PART], Z_STEP), (chunk[PART:], Y_STEP)):
        after, before = shift(part, ring, 1), shift(part, ring, -1)
        around.append((after, before))
        pairs.append(jnp.stack([part, after]))
    near = [[shift(x, r, d) for d in (1, -1)] for x, r in zip(pairs, rings)]
    known, _ = lax.optimization_barrier((known, pairs))
    state = cholesky_first(known)
    reach = []
    for (after, before), ring in zip(around, (Z_STEP, Y_STEP)):
        reach.append([shift(after[:half], ring, 1), shift(before[half:], ring, -1)])
    reach, state = lax.optimization_barrier((reach, state))
    ends = [jnp.stack([jnp.concatenate(far), before]) for far, (_, before) in zip(reach, around)]
    rest = [[shift(x, r, d) for d in (1, -1)] for x, r in zip(ends, rings)]
    near, state, _ = lax.optimization_barrier((near, state, ends))
    near_far = [shift(x[0], r, 1) for x, r in zip(near, rings)]
    weight, top = cholesky_last(place, state)
    rest, weight = lax.optimization_barrier((rest, weight))
    rest_far = [shift(x[1], r, -1) for x, r in zip(rest, rings)]
    arrived = known[:, 16:]
    arrived = arrived.reshape(PROWS, PCOLS, 16, BS).transpose(2, 1, 0, 3).reshape(16, BS, BS)
    first, second = [
        [pairs[i], ends[i], near[i][0], rest[i][0], near_far[i], rest_far[i], near[i][1], rest[i][1]]
        for i in range(2)
    ]
    result = update(place, which, weight, top, arrived, first, second, blocks)
    return result.reshape(front.shape)


def solution(mesh):
    return jax.shard_map(
        on_device,
        mesh=mesh,
        in_specs=(
            P(None, "prow", None, None, "pcol", None),
            P(None, None, "prow", None, "pcol", None),
            P(),
            P(),
        ),
        out_specs=P(None, "prow", None, None, "pcol", None),
        check_vma=False,
    )
```

```python
import functools

import jax
import jax.numpy as jnp
from jax import lax
from jax.experimental import pallas as pl
from jax.experimental.pallas import tpu as pltpu
from jax.sharding import PartitionSpec as P

BS = 128
TOP = 4
PROWS = 8
PCOLS = 16
SUB = 32
GROUP = 10
PART = 30
WIDE = 32
BOTH = ("prow", "pcol")
NN = (((1,), (0,)), ((), ()))
NT = (((1,), (1,)), ((), ()))
TN = (((0,), (0,)), ((), ()))
VMEM_LIMIT = 48 << 20


def vmem():
    return pl.BlockSpec(memory_space=pltpu.VMEM)


def smem():
    return pl.BlockSpec(memory_space=pltpu.SMEM)


def params():
    return pltpu.CompilerParams(vmem_limit_bytes=VMEM_LIMIT)


def exact_dot(a, b, dims=NN):
    return lax.dot_general(
        a, b, dims, precision=lax.Precision.HIGHEST, preferred_element_type=jnp.float32
    )


def route_kernel(col_ref, table_ref, got_ref, panel_ref, mixed_ref, inverse, pack):
    for c in range(2):
        for q in range(PCOLS):
            inverse[c, col_ref[c, q]] = q
    out_id = lax.broadcasted_iota(jnp.int32, (64, 64), 0)
    in_id = lax.broadcasted_iota(jnp.int32, (64, 64), 1)
    wanted = lax.broadcasted_iota(jnp.int32, (16, 64), 0)
    sums = [
        jnp.concatenate([got_ref[:, k, 16 + s, :] for s in range(2)], axis=0)
        for k in range(TOP)
    ]
    for c in range(2):
        table = table_ref[c : c + 1, :]
        move = (out_id % 8 == in_id // 8) & (out_id // 8 == jnp.broadcast_to(table, (64, 64)) % 8)
        move = move.astype(jnp.float32)
        pick = (wanted == jnp.broadcast_to(table, (16, 64))).astype(jnp.float32)
        for q in range(PCOLS):
            source = inverse[c, q]
            rows = got_ref[:, source, 8 * c : 8 * c + 8, :].reshape(64, BS)
            moved = exact_dot(move, rows).reshape(8, 8, BS)
            if q < TOP:
                sums[q] = sums[q] + exact_dot(pick, rows)
                panel_ref[q, :, 8 * c : 8 * c + 8, :] = moved
                mixed_ref[:, q, 16 + 8 * c : 24 + 8 * c, :] = jnp.zeros_like(moved)
            else:
                mixed_ref[:, q, 16 + 8 * c : 24 + 8 * c, :] = moved
    pack[...] = jnp.zeros_like(pack)
    place = 0
    for t in range(TOP):
        for k in range(t + 1):
            pack[place : place + 1, :] = sums[k][t : t + 1, :]
            place += 1
    for q in range(PCOLS):
        for k in range(TOP):
            pack[place + k : place + k + 1, :] = sums[k][q : q + 1, :]
        mixed_ref[:, q, :16] = jnp.broadcast_to(pack[...][None], (PROWS, 16, BS))


def route(col_map, table, got):
    return pl.pallas_call(
        route_kernel,
        out_shape=(
            jax.ShapeDtypeStruct((TOP, PROWS, 16, BS), jnp.float32),
            jax.ShapeDtypeStruct((PROWS, PCOLS, WIDE, BS), jnp.float32),
        ),
        in_specs=[smem(), vmem(), vmem()],
        out_specs=[vmem(), vmem()],
        scratch_shapes=[pltpu.SMEM((2, PCOLS), jnp.int32), pltpu.VMEM((16, BS), jnp.float32)],
        compiler_params=params(),
        name="route",
    )(col_map, table, got)


def factor_block(tab, up, width):
    for k0 in range(0, BS, width):
        rows = [jnp.broadcast_to(tab[k0 + i : k0 + i + 1, :], (8, 2 * BS)) for i in range(width)]
        a = [
            [jnp.broadcast_to(rows[i][:, k0 + j : k0 + j + 1], (8, BS)) for j in range(i + 1)]
            for i in range(width)
        ]
        scale = [None] * width
        for j in range(width):
            scale[j] = lax.rsqrt(a[j][j])
            for i in range(j + 1, width):
                a[i][j] = a[i][j] * scale[j]
            for i in range(j + 1, width):
                for m in range(j + 1, i + 1):
                    a[i][m] = a[i][m] - a[i][j] * a[m][j]
        done = []
        for i in range(width):
            halves = []
            for h in range(2):
                u = rows[i][:, h * BS : (h + 1) * BS]
                for j in range(i):
                    u = u - a[i][j] * done[j][h]
                halves.append(u * scale[i])
            done.append(halves)
            up[k0 + i : k0 + i + 1, 0:BS] = halves[0][0:1]
            up[k0 + i : k0 + i + 1, BS:] = halves[1][0:1]
        after = k0 + width
        if after < BS:
            panel = up[k0:after, :]
            tab[after:, :] = tab[after:, :] - exact_dot(panel[:, :BS], panel, TN)[after:, :]


def load(got_ref, place, work, row, col):
    for yz in range(PCOLS):
        rows = got_ref[pl.ds(yz * WIDE + place, PROWS, stride=PCOLS * WIDE), :]
        work[row + 8 * yz : row + 8 * yz + 8, col : col + BS] = rows


def cholesky_steps(steps, width, work, diagonal, inverses, tab, up):
    row = lax.broadcasted_iota(jnp.int32, (BS, BS), 0)
    col = lax.broadcasted_iota(jnp.int32, (BS, BS), 1)
    for k in steps:
        lo, hi = k * BS, (k + 1) * BS
        block = work[lo:hi, lo:hi]
        tab[:, :BS] = jnp.where(row >= col, block, block.T)
        tab[:, BS:] = (row == col).astype(jnp.float32)
        factor_block(tab, up, width)
        diagonal[lo:hi, :] = jnp.where(row >= col, up[:, :BS].T, 0.0)
        inverse = up[:, BS:]
        inverses[lo:hi, :] = inverse
        below = exact_dot(work[hi:, lo:hi], inverse, NT)
        work[hi:, lo:hi] = below
        if k + 1 < TOP:
            work[hi:, hi:] = work[hi:, hi:] - exact_dot(below, below[: (TOP - 1 - k) * BS], NT)


def first_kernel(width, steps, got_ref, work, diagonal, inverses, tab, up):
    place = 0
    for t in range(TOP):
        for k in range(t + 1):
            load(got_ref, place, work, t * BS, k * BS)
            place += 1
        for k in range(t + 1, TOP):
            work[t * BS : (t + 1) * BS, k * BS : (k + 1) * BS] = jnp.zeros((BS, BS), jnp.float32)
    for k in range(TOP):
        load(got_ref, place + k, work, TOP * BS, k * BS)
    diagonal[...] = jnp.zeros_like(diagonal)
    inverses[...] = jnp.zeros_like(inverses)
    cholesky_steps(steps, width, work, diagonal, inverses, tab, up)


def last_kernel(width, steps, place_ref, work, diagonal, inverses, weight_ref, top_ref, tab, up):
    cholesky_steps(steps, width, work, diagonal, inverses, tab, up)
    row = lax.broadcasted_iota(jnp.int32, (BS, BS), 0)
    col = lax.broadcasted_iota(jnp.int32, (BS, BS), 1)
    eye = (row == col).astype(jnp.float32)
    my_row = place_ref[0]
    my_col = place_ref[1]
    for k in reversed(range(TOP)):
        lo, hi = k * BS, (k + 1) * BS
        solved = work[TOP * BS :, lo:hi].T
        rhs = jnp.where(my_col >= TOP, solved, jnp.where(my_col == k, -eye, 0.0))
        if k + 1 < TOP:
            rhs = rhs - exact_dot(work[hi : TOP * BS, lo:hi], weight_ref[hi:, :], TN)
        weight_ref[lo:hi, :] = exact_dot(inverses[lo:hi, :], rhs, TN)
    r0 = pl.multiple_of(jnp.minimum(my_row, TOP - 1) * BS, BS)
    c0 = pl.multiple_of(jnp.minimum(my_col, TOP - 1) * BS, BS)
    found = jnp.where(my_row > my_col, work[pl.ds(r0, BS), pl.ds(c0, BS)], 0.0)
    top_ref[...] = jnp.where(my_row == my_col, diagonal[pl.ds(r0, BS), :], found)


STATE = (((TOP + 1) * BS, TOP * BS), (TOP * BS, BS), (TOP * BS, BS))


def factor_scratch():
    return [pltpu.VMEM((BS, 2 * BS), jnp.float32)] * 2


def cholesky_first(got):
    return pl.pallas_call(
        functools.partial(first_kernel, 16, (0, 1)),
        out_shape=[jax.ShapeDtypeStruct(s, jnp.float32) for s in STATE],
        in_specs=[vmem()],
        out_specs=[vmem()] * 3,
        scratch_shapes=factor_scratch(),
        compiler_params=params(),
        cost_estimate=pl.CostEstimate(flops=15 * 10**9, bytes_accessed=4 << 20, transcendentals=0),
        name="cholesky_first",
    )(got.reshape(BS * WIDE, BS))


def cholesky_last(place, state):
    def kernel(place_ref, w_in, d_in, i_in, weight_ref, top_ref, work, diagonal, inverses, tab, up):
        work[...] = w_in[...]
        diagonal[...] = d_in[...]
        inverses[...] = i_in[...]
        last_kernel(16, (2, 3), place_ref, work, diagonal, inverses, weight_ref, top_ref, tab, up)

    return pl.pallas_call(
        kernel,
        out_shape=(
            jax.ShapeDtypeStruct((TOP * BS, BS), jnp.float32),
            jax.ShapeDtypeStruct((BS, BS), jnp.float32),
        ),
        in_specs=[smem()] + [vmem()] * 3,
        out_specs=[vmem(), vmem()],
        scratch_shapes=[pltpu.VMEM(s, jnp.float32) for s in STATE] + factor_scratch(),
        compiler_params=params(),
        cost_estimate=pl.CostEstimate(flops=15 * 10**9, bytes_accessed=4 << 20, transcendentals=0),
        name="cholesky_last",
    )(place, *state)


def assemble_kernel(place_ref, slot_ref, f0, f1, f3, low, high, child_ref, out_ref):
    half = low.shape[0]
    first = jnp.where(place_ref[1] < TOP, f0[...], f1[...] + f3[...])
    out_ref[:half] = first[:half] + low[...]
    out_ref[half:] = first[half:] + high[...]
    for i in range(16):
        slot = slot_ref[i]
        out_ref[slot] = out_ref[slot] + child_ref[:, i, :]


def assemble(place, slots, *parts):
    return pl.pallas_call(
        assemble_kernel,
        out_shape=jax.ShapeDtypeStruct(parts[0].shape, jnp.float32),
        in_specs=[smem(), smem()] + [vmem()] * 6,
        out_specs=vmem(),
        compiler_params=params(),
        name="assemble",
    )(place, slots, *parts)


ORDER = (0, 1, 3, 2)


def split(x):
    big = x.astype(jnp.bfloat16)
    return big, (x - big.astype(jnp.float32)).astype(jnp.bfloat16)


def set_weights(place_ref, weight_ref, high, wide):
    my_z = place_ref[1] % 4
    for at, dz in enumerate(ORDER):
        start = pl.multiple_of((my_z + 4 - dz) % 4 * BS, BS)
        big, small = split(weight_ref[pl.ds(start, BS), :])
        high[at * BS : (at + 1) * BS, :] = big
        wide[at * BS : (at + 1) * BS, :BS] = big
        wide[at * BS : (at + 1) * BS, BS:] = small


def product(parts, high, wide):
    panel = jnp.concatenate([x.reshape(GROUP * SUB, BS) for x in parts], axis=1)
    big, small = split(panel)
    one = lax.dot_general(big, wide, NN, preferred_element_type=jnp.float32)
    two = lax.dot_general(small, high, NN, preferred_element_type=jnp.float32)
    return (one[:, :BS] + (one[:, BS:] + two)).reshape(GROUP, SUB, BS)


def chunk_rows(place_ref, dy):
    return pl.ds(pl.multiple_of((place_ref[1] // 4 + 4 - dy) % 4 * SUB, SUB), SUB)


def near_kernel(steps, place_ref, which_ref, weight_ref, top_ref, child_ref, *refs):
    first, second, (front_ref, out_ref, high, wide) = refs[:6], refs[6:12], refs[12:]
    step = pl.program_id(0)
    mine = place_ref[1] >= TOP

    @pl.when(step == 0)
    def _():
        set_weights(place_ref, weight_ref, high, wide)

    @pl.when(step < steps)
    def _():
        for dy in range(4):
            rows = chunk_rows(place_ref, dy)
            base = jnp.where(mine, front_ref[:, rows, :], 0.0)
            if dy == 2:
                out_ref[:, rows, :] = base
            else:
                at = 2 * ORDER.index(dy)
                parts = [first[at + dz // 2][dz % 2] for dz in ORDER]
                out_ref[:, rows, :] = base - product(parts, high[...], wide[...])

    @pl.when(step >= steps)
    def _():
        for dy in range(4):
            rows = chunk_rows(place_ref, dy)
            base = jnp.where(mine, front_ref[:, rows, :], 0.0)
            parts = [second[2 * at + dy // 2][dy % 2] for at in range(3)]
            out_ref[:, rows, :] = base - product(parts, high[: 3 * BS], wide[: 3 * BS])

    @pl.when(mine)
    def _():
        for i in range(GROUP):
            for c in range(2):
                source = which_ref[c, step * GROUP + i]

                @pl.when(source >= 0)
                def _():
                    out_ref[i] = out_ref[i] + child_ref[jnp.maximum(source, 0)]

    @pl.when((step == 0) & (place_ref[0] < TOP))
    def _():
        out_ref[0] = top_ref[...]


def far_kernel(steps, place_ref, weight_ref, a_low, a_high, b_low, b_high, prev_ref, out_ref, high, wide):
    step = pl.program_id(0)

    @pl.when(step == 0)
    def _():
        set_weights(place_ref, weight_ref, high, wide)

    out_ref[...] = prev_ref[...]

    @pl.when(step < steps)
    def _():
        rows = chunk_rows(place_ref, 2)
        parts = [(a_low, a_high)[dz // 2][dz % 2] for dz in ORDER]
        out_ref[:, rows, :] = prev_ref[:, rows, :] - product(parts, high[...], wide[...])

    @pl.when(step >= steps)
    def _():
        for dy in range(4):
            rows = chunk_rows(place_ref, dy)
            parts = [(b_low, b_high)[dy // 2][dy % 2]]
            out_ref[:, rows, :] = prev_ref[:, rows, :] - product(parts, high[3 * BS :], wide[3 * BS :])

    @pl.when((step == 0) & (place_ref[0] < TOP))
    def _():
        out_ref[0] = prev_ref[0]


def piece_specs(first, second):
    steps = PART // GROUP
    early = lambda i: (0, jnp.minimum(i, steps - 1), 0, 0)
    late = lambda i: (0, jnp.maximum(i - steps, 0), 0, 0)
    specs = [pl.BlockSpec((2, GROUP, SUB, BS), early) for _ in first]
    return specs + [pl.BlockSpec((2, GROUP, SUB, BS), late) for _ in second]


def weight_scratch():
    return [pltpu.VMEM((TOP * BS, BS), jnp.bfloat16), pltpu.VMEM((TOP * BS, 2 * BS), jnp.bfloat16)]


def near_update(place, which, weight, top, child, first, second, front):
    block = pl.BlockSpec((GROUP, BS, BS), lambda i: (i, 0, 0))
    return pl.pallas_call(
        functools.partial(near_kernel, PART // GROUP),
        out_shape=jax.ShapeDtypeStruct(front.shape, jnp.float32),
        grid=(pl.cdiv(front.shape[0], GROUP),),
        in_specs=[smem(), smem(), vmem(), vmem(), vmem()] + piece_specs(first, second) + [block],
        out_specs=block,
        scratch_shapes=weight_scratch(),
        compiler_params=params(),
        cost_estimate=pl.CostEstimate(flops=10**10, bytes_accessed=20 << 20, transcendentals=0),
        name="near_update",
    )(place, which, weight, top, child, *first, *second, front)


def far_update(place, weight, first, second, result):
    block = pl.BlockSpec((GROUP, BS, BS), lambda i: (i, 0, 0))
    return pl.pallas_call(
        functools.partial(far_kernel, PART // GROUP),
        out_shape=jax.ShapeDtypeStruct(result.shape, jnp.float32),
        grid=(pl.cdiv(result.shape[0], GROUP),),
        in_specs=[smem(), vmem()] + piece_specs(first, second) + [block],
        out_specs=block,
        input_output_aliases={6: 0},
        scratch_shapes=weight_scratch(),
        compiler_params=params(),
        cost_estimate=pl.CostEstimate(flops=3 * 10**9, bytes_accessed=12 << 20, transcendentals=0),
        name="far_update",
    )(place, weight, *first, *second, result)


Y_STEP = 4
Z_STEP = 1


def shift(x, axis, by):
    if axis == Y_STEP:
        pairs = [(4 * y + z, 4 * ((y + by) % 4) + z) for y in range(4) for z in range(4)]
    else:
        pairs = [(4 * y + z, 4 * y + (z + by) % 4) for y in range(4) for z in range(4)]
    return lax.ppermute(x, "pcol", pairs)


SAME_Y = [[p * PCOLS + 4 * y + z for z in range(4) for p in range(PROWS)] for y in range(4)]


def hop(x, origin, target):
    return lax.ppermute(x, "pcol", [(4 * origin + z, 4 * target + z) for z in range(4)])


def on_device(front, child, row_map, col_map):
    count = front.shape[0]
    row_here = lax.axis_index("prow")
    col_here = lax.axis_index("pcol")
    place = jnp.stack([row_here, col_here]).astype(jnp.int32)
    blocks = front.reshape(count, BS, BS)
    pieces = child.reshape(16, BS, BS)
    by_source = row_map.reshape(2, 8, PROWS).transpose(0, 2, 1)
    table = by_source.reshape(2, 64)
    mine = by_source % PROWS == row_here
    slots = jnp.sum(jnp.where(mine, by_source // PROWS, 0), axis=2)
    padded = pl.cdiv(count, GROUP) * GROUP
    hit = slots[:, :, None] == jnp.arange(padded)[None, None, :]
    which = jnp.max(jnp.where(hit, jnp.arange(16).reshape(2, 8, 1), -1), axis=1)
    cuts = [blocks[:, y * SUB : (y + 1) * SUB] for y in range(4)]
    half = count // 2
    relay = [hop(cuts[2][:half], 0, 1), hop(cuts[2][half:], 0, 3)]
    sent = [hop(cuts[1], 0, 1), hop(cuts[3], 0, 3)]
    first = jnp.concatenate([pieces, blocks[:2], jnp.zeros((6, BS, BS), jnp.float32)])
    first = first.reshape(24, PCOLS, PROWS, BS).transpose(2, 1, 0, 3).reshape(BS, 24, BS)
    got = lax.all_to_all(first, BOTH, 0, 0, tiled=True)
    got, relay = lax.optimization_barrier((got, relay))
    sent = sent + [hop(relay[0], 1, 2), hop(relay[1], 3, 2)]
    panel, mixed = route(col_map, table, got.reshape(PROWS, PCOLS, 24, BS))
    panel = lax.all_to_all(
        panel.reshape(4 * PROWS, 16, BS), BOTH, 0, 0, tiled=True, axis_index_groups=SAME_Y
    )
    chunk = assemble(place, slots.reshape(16), cuts[0], *sent, panel)
    chunk, mixed = lax.optimization_barrier((chunk, mixed))
    known = lax.all_to_all(mixed.reshape(BS, WIDE, BS), BOTH, 0, 0, tiled=True)
    half = PART // 2
    rings = (Y_STEP, Z_STEP)
    around, pairs = [], []
    for part, ring in ((chunk[:PART], Z_STEP), (chunk[PART:], Y_STEP)):
        after, before = shift(part, ring, 1), shift(part, ring, -1)
        around.append((after, before))
        pairs.append(jnp.stack([part, after]))
    near = [[shift(x, r, d) for d in (1, -1)] for x, r in zip(pairs, rings)]
    known, _ = lax.optimization_barrier((known, pairs))
    state = cholesky_first(known)
    reach = []
    for (after, before), ring in zip(around, (Z_STEP, Y_STEP)):
        reach.append([shift(after[:half], ring, 1), shift(before[half:], ring, -1)])
    reach, state = lax.optimization_barrier((reach, state))
    ends = [jnp.stack([jnp.concatenate(far), before]) for far, (_, before) in zip(reach, around)]
    rest = [[shift(x, r, d) for d in (1, -1)] for x, r in zip(ends, rings)]
    near, state, _ = lax.optimization_barrier((near, state, ends))
    near_far = [shift(x[0], r, 1) for x, r in zip(near, rings)]
    weight, top = cholesky_last(place, state)
    rest, weight = lax.optimization_barrier((rest, weight))
    rest_far = [shift(x[1], r, -1) for x, r in zip(rest, rings)]
    arrived = known[:, 16:]
    arrived = arrived.reshape(PROWS, PCOLS, 16, BS).transpose(2, 1, 0, 3).reshape(16, BS, BS)
    first, second = [
        [pairs[i], ends[i], near[i][0], rest[i][0], near[i][1], rest[i][1]] for i in range(2)
    ]
    result = near_update(place, which, weight, top, arrived, first, second, blocks)
    first, second = [[near_far[i], rest_far[i]] for i in range(2)]
    result = far_update(place, weight, first, second, result)
    return result.reshape(front.shape)


def solution(mesh):
    return jax.shard_map(
        on_device,
        mesh=mesh,
        in_specs=(
            P(None, "prow", None, None, "pcol", None),
            P(None, None, "prow", None, "pcol", None),
            P(),
            P(),
        ),
        out_specs=P(None, "prow", None, None, "pcol", None),
        check_vma=False,
    )
```

```python
import functools

import jax
import jax.numpy as jnp
from jax import lax
from jax.experimental import pallas as pl
from jax.experimental.pallas import tpu as pltpu
from jax.sharding import PartitionSpec as P

BS = 128
TOP = 4
PROWS = 8
PCOLS = 16
SUB = 32
GROUP = 10
PART = 30
WIDE = 32
BOTH = ("prow", "pcol")
NN = (((1,), (0,)), ((), ()))
NT = (((1,), (1,)), ((), ()))
TN = (((0,), (0,)), ((), ()))
VMEM_LIMIT = 48 << 20


def vmem():
    return pl.BlockSpec(memory_space=pltpu.VMEM)


def smem():
    return pl.BlockSpec(memory_space=pltpu.SMEM)


def params():
    return pltpu.CompilerParams(vmem_limit_bytes=VMEM_LIMIT)


def exact_dot(a, b, dims=NN):
    return lax.dot_general(
        a, b, dims, precision=lax.Precision.HIGHEST, preferred_element_type=jnp.float32
    )


def route_kernel(col_ref, table_ref, got_ref, panel_ref, mixed_ref, inverse, pack):
    for c in range(2):
        for q in range(PCOLS):
            inverse[c, col_ref[c, q]] = q
    out_id = lax.broadcasted_iota(jnp.int32, (64, 64), 0)
    in_id = lax.broadcasted_iota(jnp.int32, (64, 64), 1)
    wanted = lax.broadcasted_iota(jnp.int32, (16, 64), 0)
    sums = [
        jnp.concatenate([got_ref[:, k, 16 + s, :] for s in range(2)], axis=0)
        for k in range(TOP)
    ]
    for c in range(2):
        table = table_ref[c : c + 1, :]
        move = (out_id % 8 == in_id // 8) & (out_id // 8 == jnp.broadcast_to(table, (64, 64)) % 8)
        move = move.astype(jnp.float32)
        pick = (wanted == jnp.broadcast_to(table, (16, 64))).astype(jnp.float32)
        for q in range(PCOLS):
            source = inverse[c, q]
            rows = got_ref[:, source, 8 * c : 8 * c + 8, :].reshape(64, BS)
            moved = exact_dot(move, rows).reshape(8, 8, BS)
            if q < TOP:
                sums[q] = sums[q] + exact_dot(pick, rows)
                panel_ref[q, :, 8 * c : 8 * c + 8, :] = moved
                mixed_ref[:, q, 16 + 8 * c : 24 + 8 * c, :] = jnp.zeros_like(moved)
            else:
                mixed_ref[:, q, 16 + 8 * c : 24 + 8 * c, :] = moved
    pack[...] = jnp.zeros_like(pack)
    place = 0
    for t in range(TOP):
        for k in range(t + 1):
            pack[place : place + 1, :] = sums[k][t : t + 1, :]
            place += 1
    for q in range(PCOLS):
        for k in range(TOP):
            pack[place + k : place + k + 1, :] = sums[k][q : q + 1, :]
        mixed_ref[:, q, :16] = jnp.broadcast_to(pack[...][None], (PROWS, 16, BS))


def route(col_map, table, got):
    return pl.pallas_call(
        route_kernel,
        out_shape=(
            jax.ShapeDtypeStruct((TOP, PROWS, 16, BS), jnp.float32),
            jax.ShapeDtypeStruct((PROWS, PCOLS, WIDE, BS), jnp.float32),
        ),
        in_specs=[smem(), vmem(), vmem()],
        out_specs=[vmem(), vmem()],
        scratch_shapes=[pltpu.SMEM((2, PCOLS), jnp.int32), pltpu.VMEM((16, BS), jnp.float32)],
        compiler_params=params(),
        name="route",
    )(col_map, table, got)


def factor_block(tab, up, width):
    for k0 in range(0, BS, width):
        rows = [jnp.broadcast_to(tab[k0 + i : k0 + i + 1, :], (8, 2 * BS)) for i in range(width)]
        a = [
            [jnp.broadcast_to(rows[i][:, k0 + j : k0 + j + 1], (8, BS)) for j in range(i + 1)]
            for i in range(width)
        ]
        scale = [None] * width
        for j in range(width):
            scale[j] = lax.rsqrt(a[j][j])
            for i in range(j + 1, width):
                a[i][j] = a[i][j] * scale[j]
            for i in range(j + 1, width):
                for m in range(j + 1, i + 1):
                    a[i][m] = a[i][m] - a[i][j] * a[m][j]
        done = []
        for i in range(width):
            halves = []
            for h in range(2):
                u = rows[i][:, h * BS : (h + 1) * BS]
                for j in range(i):
                    u = u - a[i][j] * done[j][h]
                halves.append(u * scale[i])
            done.append(halves)
            up[k0 + i : k0 + i + 1, 0:BS] = halves[0][0:1]
            up[k0 + i : k0 + i + 1, BS:] = halves[1][0:1]
        after = k0 + width
        if after < BS:
            panel = up[k0:after, :]
            tab[after:, :] = tab[after:, :] - exact_dot(panel[:, :BS], panel, TN)[after:, :]


def load(got_ref, place, work, row, col):
    for yz in range(PCOLS):
        rows = got_ref[pl.ds(yz * WIDE + place, PROWS, stride=PCOLS * WIDE), :]
        work[row + 8 * yz : row + 8 * yz + 8, col : col + BS] = rows


def cholesky_steps(steps, width, work, diagonal, inverses, tab, up):
    row = lax.broadcasted_iota(jnp.int32, (BS, BS), 0)
    col = lax.broadcasted_iota(jnp.int32, (BS, BS), 1)
    for k in steps:
        lo, hi = k * BS, (k + 1) * BS
        block = work[lo:hi, lo:hi]
        tab[:, :BS] = jnp.where(row >= col, block, block.T)
        tab[:, BS:] = (row == col).astype(jnp.float32)
        factor_block(tab, up, width)
        diagonal[lo:hi, :] = jnp.where(row >= col, up[:, :BS].T, 0.0)
        inverse = up[:, BS:]
        inverses[lo:hi, :] = inverse
        below = exact_dot(work[hi:, lo:hi], inverse, NT)
        work[hi:, lo:hi] = below
        if k + 1 < TOP:
            work[hi:, hi:] = work[hi:, hi:] - exact_dot(below, below[: (TOP - 1 - k) * BS], NT)


def first_kernel(width, steps, got_ref, work, diagonal, inverses, tab, up):
    place = 0
    for t in range(TOP):
        for k in range(t + 1):
            load(got_ref, place, work, t * BS, k * BS)
            place += 1
        for k in range(t + 1, TOP):
            work[t * BS : (t + 1) * BS, k * BS : (k + 1) * BS] = jnp.zeros((BS, BS), jnp.float32)
    for k in range(TOP):
        load(got_ref, place + k, work, TOP * BS, k * BS)
    diagonal[...] = jnp.zeros_like(diagonal)
    inverses[...] = jnp.zeros_like(inverses)
    cholesky_steps(steps, width, work, diagonal, inverses, tab, up)


def last_kernel(width, steps, place_ref, work, diagonal, inverses, weight_ref, top_ref, tab, up):
    cholesky_steps(steps, width, work, diagonal, inverses, tab, up)
    row = lax.broadcasted_iota(jnp.int32, (BS, BS), 0)
    col = lax.broadcasted_iota(jnp.int32, (BS, BS), 1)
    eye = (row == col).astype(jnp.float32)
    my_row = place_ref[0]
    my_col = place_ref[1]
    for k in reversed(range(TOP)):
        lo, hi = k * BS, (k + 1) * BS
        solved = work[TOP * BS :, lo:hi].T
        rhs = jnp.where(my_col >= TOP, solved, jnp.where(my_col == k, -eye, 0.0))
        if k + 1 < TOP:
            rhs = rhs - exact_dot(work[hi : TOP * BS, lo:hi], weight_ref[hi:, :], TN)
        weight_ref[lo:hi, :] = exact_dot(inverses[lo:hi, :], rhs, TN)
    r0 = pl.multiple_of(jnp.minimum(my_row, TOP - 1) * BS, BS)
    c0 = pl.multiple_of(jnp.minimum(my_col, TOP - 1) * BS, BS)
    found = jnp.where(my_row > my_col, work[pl.ds(r0, BS), pl.ds(c0, BS)], 0.0)
    top_ref[...] = jnp.where(my_row == my_col, diagonal[pl.ds(r0, BS), :], found)


STATE = (((TOP + 1) * BS, TOP * BS), (TOP * BS, BS), (TOP * BS, BS))


def factor_scratch():
    return [pltpu.VMEM((BS, 2 * BS), jnp.float32)] * 2


def cholesky_first(got):
    return pl.pallas_call(
        functools.partial(first_kernel, 16, (0, 1)),
        out_shape=[jax.ShapeDtypeStruct(s, jnp.float32) for s in STATE],
        in_specs=[vmem()],
        out_specs=[vmem()] * 3,
        scratch_shapes=factor_scratch(),
        compiler_params=params(),
        cost_estimate=pl.CostEstimate(flops=15 * 10**9, bytes_accessed=4 << 20, transcendentals=0),
        name="cholesky_first",
    )(got.reshape(BS * WIDE, BS))


def cholesky_last(place, state):
    def kernel(place_ref, w_in, d_in, i_in, weight_ref, top_ref, work, diagonal, inverses, tab, up):
        work[...] = w_in[...]
        diagonal[...] = d_in[...]
        inverses[...] = i_in[...]
        last_kernel(16, (2, 3), place_ref, work, diagonal, inverses, weight_ref, top_ref, tab, up)

    return pl.pallas_call(
        kernel,
        out_shape=(
            jax.ShapeDtypeStruct((TOP * BS, BS), jnp.float32),
            jax.ShapeDtypeStruct((BS, BS), jnp.float32),
        ),
        in_specs=[smem()] + [vmem()] * 3,
        out_specs=[vmem(), vmem()],
        scratch_shapes=[pltpu.VMEM(s, jnp.float32) for s in STATE] + factor_scratch(),
        compiler_params=params(),
        cost_estimate=pl.CostEstimate(flops=15 * 10**9, bytes_accessed=4 << 20, transcendentals=0),
        name="cholesky_last",
    )(place, *state)


def assemble_kernel(place_ref, slot_ref, f0, f1, f3, low, high, child_ref, out_ref):
    half = low.shape[0]
    first = jnp.where(place_ref[1] < TOP, f0[...], f1[...] + f3[...])
    out_ref[:half] = first[:half] + low[...]
    out_ref[half:] = first[half:] + high[...]
    for i in range(16):
        slot = slot_ref[i]
        out_ref[slot] = out_ref[slot] + child_ref[:, i, :]


def assemble(place, slots, *parts):
    return pl.pallas_call(
        assemble_kernel,
        out_shape=jax.ShapeDtypeStruct(parts[0].shape, jnp.float32),
        in_specs=[smem(), smem()] + [vmem()] * 6,
        out_specs=vmem(),
        compiler_params=params(),
        name="assemble",
    )(place, slots, *parts)


ORDER = (0, 1, 3, 2)


def split(x):
    big = x.astype(jnp.bfloat16)
    return big, (x - big.astype(jnp.float32)).astype(jnp.bfloat16)


def set_weights(place_ref, weight_ref, high, wide):
    my_z = place_ref[1] % 4
    for at, dz in enumerate(ORDER):
        start = pl.multiple_of((my_z + 4 - dz) % 4 * BS, BS)
        big, small = split(weight_ref[pl.ds(start, BS), :])
        high[at * BS : (at + 1) * BS, :] = big
        wide[at * BS : (at + 1) * BS, :BS] = big
        wide[at * BS : (at + 1) * BS, BS:] = small


def product(parts, high, wide):
    panel = jnp.concatenate([x.reshape(GROUP * SUB, BS) for x in parts], axis=1)
    big, small = split(panel)
    one = lax.dot_general(big, wide, NN, preferred_element_type=jnp.float32)
    two = lax.dot_general(small, high, NN, preferred_element_type=jnp.float32)
    return (one[:, :BS] + (one[:, BS:] + two)).reshape(GROUP, SUB, BS)


def chunk_rows(place_ref, dy):
    return pl.ds(pl.multiple_of((place_ref[1] // 4 + 4 - dy) % 4 * SUB, SUB), SUB)


def near_kernel(steps, place_ref, which_ref, weight_ref, top_ref, child_ref, *refs):
    first, second, (front_ref, out_ref, high, wide) = refs[:6], refs[6:12], refs[12:]
    step = pl.program_id(0)
    mine = place_ref[1] >= TOP

    @pl.when(step == 0)
    def _():
        set_weights(place_ref, weight_ref, high, wide)

    @pl.when(step < steps)
    def _():
        for dy in range(4):
            rows = chunk_rows(place_ref, dy)
            base = jnp.where(mine, front_ref[:, rows, :], 0.0)
            if dy == 2:
                out_ref[:, rows, :] = base
            else:
                at = 2 * ORDER.index(dy)
                parts = [first[at + dz // 2][dz % 2] for dz in ORDER]
                out_ref[:, rows, :] = base - product(parts, high[...], wide[...])

    @pl.when(step >= steps)
    def _():
        for dy in range(4):
            rows = chunk_rows(place_ref, dy)
            base = jnp.where(mine, front_ref[:, rows, :], 0.0)
            parts = [second[2 * at + dy // 2][dy % 2] for at in range(3)]
            out_ref[:, rows, :] = base - product(parts, high[: 3 * BS], wide[: 3 * BS])

    @pl.when(mine)
    def _():
        for i in range(GROUP):
            for c in range(2):
                source = which_ref[c, step * GROUP + i]

                @pl.when(source >= 0)
                def _():
                    out_ref[i] = out_ref[i] + child_ref[jnp.maximum(source, 0)]

    @pl.when((step == 0) & (place_ref[0] < TOP))
    def _():
        out_ref[0] = top_ref[...]


def far_kernel(steps, place_ref, weight_ref, a_low, a_high, b_low, b_high, prev_ref, out_ref, high, wide):
    step = pl.program_id(0)

    @pl.when(step == 0)
    def _():
        set_weights(place_ref, weight_ref, high, wide)

    out_ref[...] = prev_ref[...]

    @pl.when(step < steps)
    def _():
        rows = chunk_rows(place_ref, 2)
        parts = [(a_low, a_high)[dz // 2][dz % 2] for dz in ORDER]
        out_ref[:, rows, :] = prev_ref[:, rows, :] - product(parts, high[...], wide[...])

    @pl.when(step >= steps)
    def _():
        for dy in range(4):
            rows = chunk_rows(place_ref, dy)
            parts = [(b_low, b_high)[dy // 2][dy % 2]]
            out_ref[:, rows, :] = prev_ref[:, rows, :] - product(parts, high[3 * BS :], wide[3 * BS :])

    @pl.when((step == 0) & (place_ref[0] < TOP))
    def _():
        out_ref[0] = prev_ref[0]


def piece_specs(first, second):
    steps = PART // GROUP
    early = lambda i: (0, jnp.minimum(i, steps - 1), 0, 0)
    late = lambda i: (0, jnp.maximum(i - steps, 0), 0, 0)
    specs = [pl.BlockSpec((2, GROUP, SUB, BS), early) for _ in first]
    return specs + [pl.BlockSpec((2, GROUP, SUB, BS), late) for _ in second]


def weight_scratch():
    return [pltpu.VMEM((TOP * BS, BS), jnp.bfloat16), pltpu.VMEM((TOP * BS, 2 * BS), jnp.bfloat16)]


def near_update(place, which, weight, top, child, first, second, front):
    block = pl.BlockSpec((GROUP, BS, BS), lambda i: (i, 0, 0))
    return pl.pallas_call(
        functools.partial(near_kernel, PART // GROUP),
        out_shape=jax.ShapeDtypeStruct(front.shape, jnp.float32),
        grid=(pl.cdiv(front.shape[0], GROUP),),
        in_specs=[smem(), smem(), vmem(), vmem(), vmem()] + piece_specs(first, second) + [block],
        out_specs=block,
        scratch_shapes=weight_scratch(),
        compiler_params=params(),
        cost_estimate=pl.CostEstimate(flops=10**10, bytes_accessed=20 << 20, transcendentals=0),
        name="near_update",
    )(place, which, weight, top, child, *first, *second, front)


def far_update(place, weight, first, second, result):
    block = pl.BlockSpec((GROUP, BS, BS), lambda i: (i, 0, 0))
    return pl.pallas_call(
        functools.partial(far_kernel, PART // GROUP),
        out_shape=jax.ShapeDtypeStruct(result.shape, jnp.float32),
        grid=(pl.cdiv(result.shape[0], GROUP),),
        in_specs=[smem(), vmem()] + piece_specs(first, second) + [block],
        out_specs=block,
        input_output_aliases={6: 0},
        scratch_shapes=weight_scratch(),
        compiler_params=params(),
        cost_estimate=pl.CostEstimate(flops=3 * 10**9, bytes_accessed=12 << 20, transcendentals=0),
        name="far_update",
    )(place, weight, *first, *second, result)


Y_STEP = 4
Z_STEP = 1


def shift(x, axis, by):
    if axis == Y_STEP:
        pairs = [(4 * y + z, 4 * ((y + by) % 4) + z) for y in range(4) for z in range(4)]
    else:
        pairs = [(4 * y + z, 4 * y + (z + by) % 4) for y in range(4) for z in range(4)]
    return lax.ppermute(x, "pcol", pairs)


SAME_Y = [[p * PCOLS + 4 * y + z for z in range(4) for p in range(PROWS)] for y in range(4)]


def hop(x, origin, target):
    return lax.ppermute(x, "pcol", [(4 * origin + z, 4 * target + z) for z in range(4)])


def on_device(front, child, row_map, col_map):
    count = front.shape[0]
    row_here = lax.axis_index("prow")
    col_here = lax.axis_index("pcol")
    place = jnp.stack([row_here, col_here]).astype(jnp.int32)
    blocks = front.reshape(count, BS, BS)
    pieces = child.reshape(16, BS, BS)
    by_source = row_map.reshape(2, 8, PROWS).transpose(0, 2, 1)
    table = by_source.reshape(2, 64)
    mine = by_source % PROWS == row_here
    slots = jnp.sum(jnp.where(mine, by_source // PROWS, 0), axis=2)
    padded = pl.cdiv(count, GROUP) * GROUP
    hit = slots[:, :, None] == jnp.arange(padded)[None, None, :]
    which = jnp.max(jnp.where(hit, jnp.arange(16).reshape(2, 8, 1), -1), axis=1)
    cuts = [blocks[:, y * SUB : (y + 1) * SUB] for y in range(4)]
    half = count // 2
    relay = [hop(cuts[2][:half], 0, 1), hop(cuts[2][half:], 0, 3)]
    sent = [hop(cuts[1], 0, 1), hop(cuts[3], 0, 3)]
    first = jnp.concatenate([pieces, blocks[:2], jnp.zeros((6, BS, BS), jnp.float32)])
    first = first.reshape(24, PCOLS, PROWS, BS).transpose(2, 1, 0, 3).reshape(BS, 24, BS)
    got = lax.all_to_all(first, BOTH, 0, 0, tiled=True)
    got, relay = lax.optimization_barrier((got, relay))
    sent = sent + [hop(relay[0], 1, 2), hop(relay[1], 3, 2)]
    panel, mixed = route(col_map, table, got.reshape(PROWS, PCOLS, 24, BS))
    panel = lax.all_to_all(
        panel.reshape(4 * PROWS, 16, BS), BOTH, 0, 0, tiled=True, axis_index_groups=SAME_Y
    )
    chunk = assemble(place, slots.reshape(16), cuts[0], *sent, panel)
    half = PART // 2
    rings = (Y_STEP, Z_STEP)
    around, pairs = [], []
    for part, ring in ((chunk[:PART], Z_STEP), (chunk[PART:], Y_STEP)):
        after, before = shift(part, ring, 1), shift(part, ring, -1)
        around.append((after, before))
        pairs.append(jnp.stack([part, after]))
    mixed, _ = lax.optimization_barrier((mixed, around))
    known = lax.all_to_all(mixed.reshape(BS, WIDE, BS), BOTH, 0, 0, tiled=True)
    near = [[shift(x, r, d) for d in (1, -1)] for x, r in zip(pairs, rings)]
    reach = []
    for (after, before), ring in zip(around, (Z_STEP, Y_STEP)):
        reach.append([shift(after[:half], ring, 1), shift(before[half:], ring, -1)])
    known, _ = lax.optimization_barrier((known, reach))
    state = cholesky_first(known)
    reach, state = lax.optimization_barrier((reach, state))
    ends = [jnp.stack([jnp.concatenate(far), before]) for far, (_, before) in zip(reach, around)]
    rest = [[shift(x, r, d) for d in (1, -1)] for x, r in zip(ends, rings)]
    near, state, _ = lax.optimization_barrier((near, state, ends))
    near_far = [shift(x[0], r, 1) for x, r in zip(near, rings)]
    weight, top = cholesky_last(place, state)
    rest, weight = lax.optimization_barrier((rest, weight))
    rest_far = [shift(x[1], r, -1) for x, r in zip(rest, rings)]
    arrived = known[:, 16:]
    arrived = arrived.reshape(PROWS, PCOLS, 16, BS).transpose(2, 1, 0, 3).reshape(16, BS, BS)
    first, second = [
        [pairs[i], ends[i], near[i][0], rest[i][0], near[i][1], rest[i][1]] for i in range(2)
    ]
    result = near_update(place, which, weight, top, arrived, first, second, blocks)
    first, second = [[near_far[i], rest_far[i]] for i in range(2)]
    result = far_update(place, weight, first, second, result)
    return result.reshape(front.shape)


def solution(mesh):
    return jax.shard_map(
        on_device,
        mesh=mesh,
        in_specs=(
            P(None, "prow", None, None, "pcol", None),
            P(None, None, "prow", None, "pcol", None),
            P(),
            P(),
        ),
        out_specs=P(None, "prow", None, None, "pcol", None),
        check_vma=False,
    )
```

```python
import functools

import jax
import jax.numpy as jnp
from jax import lax
from jax.experimental import pallas as pl
from jax.experimental.pallas import tpu as pltpu
from jax.sharding import PartitionSpec as P

BS = 128
TOP = 4
PROWS = 8
PCOLS = 16
SUB = 32
GROUP = 10
PART = 30
WIDE = 32
BOTH = ("prow", "pcol")
NN = (((1,), (0,)), ((), ()))
NT = (((1,), (1,)), ((), ()))
TN = (((0,), (0,)), ((), ()))
VMEM_LIMIT = 48 << 20


def vmem():
    return pl.BlockSpec(memory_space=pltpu.VMEM)


def smem():
    return pl.BlockSpec(memory_space=pltpu.SMEM)


def params():
    return pltpu.CompilerParams(vmem_limit_bytes=VMEM_LIMIT)


def exact_dot(a, b, dims=NN):
    return lax.dot_general(
        a, b, dims, precision=lax.Precision.HIGHEST, preferred_element_type=jnp.float32
    )


def route_kernel(col_ref, table_ref, got_ref, panel_ref, mixed_ref, inverse, pack):
    for c in range(2):
        for q in range(PCOLS):
            inverse[c, col_ref[c, q]] = q
    out_id = lax.broadcasted_iota(jnp.int32, (64, 64), 0)
    in_id = lax.broadcasted_iota(jnp.int32, (64, 64), 1)
    wanted = lax.broadcasted_iota(jnp.int32, (16, 64), 0)
    sums = [
        jnp.concatenate([got_ref[:, k, 16 + s, :] for s in range(2)], axis=0)
        for k in range(TOP)
    ]
    for c in range(2):
        table = table_ref[c : c + 1, :]
        move = (out_id % 8 == in_id // 8) & (out_id // 8 == jnp.broadcast_to(table, (64, 64)) % 8)
        move = move.astype(jnp.float32)
        pick = (wanted == jnp.broadcast_to(table, (16, 64))).astype(jnp.float32)
        for q in range(PCOLS):
            source = inverse[c, q]
            rows = got_ref[:, source, 8 * c : 8 * c + 8, :].reshape(64, BS)
            moved = exact_dot(move, rows).reshape(8, 8, BS)
            if q < TOP:
                sums[q] = sums[q] + exact_dot(pick, rows)
                panel_ref[q, :, 8 * c : 8 * c + 8, :] = moved
                mixed_ref[:, q, 16 + 8 * c : 24 + 8 * c, :] = jnp.zeros_like(moved)
            else:
                mixed_ref[:, q, 16 + 8 * c : 24 + 8 * c, :] = moved
    pack[...] = jnp.zeros_like(pack)
    place = 0
    for t in range(TOP):
        for k in range(t + 1):
            pack[place : place + 1, :] = sums[k][t : t + 1, :]
            place += 1
    for q in range(PCOLS):
        for k in range(TOP):
            pack[place + k : place + k + 1, :] = sums[k][q : q + 1, :]
        mixed_ref[:, q, :16] = jnp.broadcast_to(pack[...][None], (PROWS, 16, BS))


def route(col_map, table, got):
    return pl.pallas_call(
        route_kernel,
        out_shape=(
            jax.ShapeDtypeStruct((TOP, PROWS, 16, BS), jnp.float32),
            jax.ShapeDtypeStruct((PROWS, PCOLS, WIDE, BS), jnp.float32),
        ),
        in_specs=[smem(), vmem(), vmem()],
        out_specs=[vmem(), vmem()],
        scratch_shapes=[pltpu.SMEM((2, PCOLS), jnp.int32), pltpu.VMEM((16, BS), jnp.float32)],
        compiler_params=params(),
        name="route",
    )(col_map, table, got)


def factor_block(tab, up, width):
    for k0 in range(0, BS, width):
        rows = [jnp.broadcast_to(tab[k0 + i : k0 + i + 1, :], (8, 2 * BS)) for i in range(width)]
        a = [
            [jnp.broadcast_to(rows[i][:, k0 + j : k0 + j + 1], (8, BS)) for j in range(i + 1)]
            for i in range(width)
        ]
        scale = [None] * width
        for j in range(width):
            scale[j] = lax.rsqrt(a[j][j])
            for i in range(j + 1, width):
                a[i][j] = a[i][j] * scale[j]
            for i in range(j + 1, width):
                for m in range(j + 1, i + 1):
                    a[i][m] = a[i][m] - a[i][j] * a[m][j]
        done = []
        for i in range(width):
            halves = []
            for h in range(2):
                u = rows[i][:, h * BS : (h + 1) * BS]
                for j in range(i):
                    u = u - a[i][j] * done[j][h]
                halves.append(u * scale[i])
            done.append(halves)
            up[k0 + i : k0 + i + 1, 0:BS] = halves[0][0:1]
            up[k0 + i : k0 + i + 1, BS:] = halves[1][0:1]
        after = k0 + width
        if after < BS:
            panel = up[k0:after, :]
            tab[after:, :] = tab[after:, :] - exact_dot(panel[:, :BS], panel, TN)[after:, :]


def load(got_ref, place, work, row, col):
    for yz in range(PCOLS):
        rows = got_ref[pl.ds(yz * WIDE + place, PROWS, stride=PCOLS * WIDE), :]
        work[row + 8 * yz : row + 8 * yz + 8, col : col + BS] = rows


def cholesky_steps(steps, width, work, diagonal, inverses, tab, up):
    row = lax.broadcasted_iota(jnp.int32, (BS, BS), 0)
    col = lax.broadcasted_iota(jnp.int32, (BS, BS), 1)
    for k in steps:
        lo, hi = k * BS, (k + 1) * BS
        block = work[lo:hi, lo:hi]
        tab[:, :BS] = jnp.where(row >= col, block, block.T)
        tab[:, BS:] = (row == col).astype(jnp.float32)
        factor_block(tab, up, width)
        diagonal[lo:hi, :] = jnp.where(row >= col, up[:, :BS].T, 0.0)
        inverse = up[:, BS:]
        inverses[lo:hi, :] = inverse
        below = exact_dot(work[hi:, lo:hi], inverse, NT)
        work[hi:, lo:hi] = below
        if k + 1 < TOP:
            work[hi:, hi:] = work[hi:, hi:] - exact_dot(below, below[: (TOP - 1 - k) * BS], NT)


def first_kernel(width, steps, got_ref, work, diagonal, inverses, tab, up):
    place = 0
    for t in range(TOP):
        for k in range(t + 1):
            load(got_ref, place, work, t * BS, k * BS)
            place += 1
        for k in range(t + 1, TOP):
            work[t * BS : (t + 1) * BS, k * BS : (k + 1) * BS] = jnp.zeros((BS, BS), jnp.float32)
    for k in range(TOP):
        load(got_ref, place + k, work, TOP * BS, k * BS)
    diagonal[...] = jnp.zeros_like(diagonal)
    inverses[...] = jnp.zeros_like(inverses)
    cholesky_steps(steps, width, work, diagonal, inverses, tab, up)


def last_kernel(width, steps, place_ref, work, diagonal, inverses, weight_ref, top_ref, tab, up):
    cholesky_steps(steps, width, work, diagonal, inverses, tab, up)
    row = lax.broadcasted_iota(jnp.int32, (BS, BS), 0)
    col = lax.broadcasted_iota(jnp.int32, (BS, BS), 1)
    eye = (row == col).astype(jnp.float32)
    my_row = place_ref[0]
    my_col = place_ref[1]
    for k in reversed(range(TOP)):
        lo, hi = k * BS, (k + 1) * BS
        solved = work[TOP * BS :, lo:hi].T
        rhs = jnp.where(my_col >= TOP, solved, jnp.where(my_col == k, -eye, 0.0))
        if k + 1 < TOP:
            rhs = rhs - exact_dot(work[hi : TOP * BS, lo:hi], weight_ref[hi:, :], TN)
        weight_ref[lo:hi, :] = exact_dot(inverses[lo:hi, :], rhs, TN)
    r0 = pl.multiple_of(jnp.minimum(my_row, TOP - 1) * BS, BS)
    c0 = pl.multiple_of(jnp.minimum(my_col, TOP - 1) * BS, BS)
    found = jnp.where(my_row > my_col, work[pl.ds(r0, BS), pl.ds(c0, BS)], 0.0)
    top_ref[...] = jnp.where(my_row == my_col, diagonal[pl.ds(r0, BS), :], found)


STATE = (((TOP + 1) * BS, TOP * BS), (TOP * BS, BS), (TOP * BS, BS))


def factor_scratch():
    return [pltpu.VMEM((BS, 2 * BS), jnp.float32)] * 2


def cholesky_first(got):
    return pl.pallas_call(
        functools.partial(first_kernel, 16, (0, 1)),
        out_shape=[jax.ShapeDtypeStruct(s, jnp.float32) for s in STATE],
        in_specs=[vmem()],
        out_specs=[vmem()] * 3,
        scratch_shapes=factor_scratch(),
        compiler_params=params(),
        cost_estimate=pl.CostEstimate(flops=15 * 10**9, bytes_accessed=4 << 20, transcendentals=0),
        name="cholesky_first",
    )(got.reshape(BS * WIDE, BS))


def cholesky_last(place, state):
    def kernel(place_ref, w_in, d_in, i_in, weight_ref, top_ref, work, diagonal, inverses, tab, up):
        work[...] = w_in[...]
        diagonal[...] = d_in[...]
        inverses[...] = i_in[...]
        last_kernel(16, (2, 3), place_ref, work, diagonal, inverses, weight_ref, top_ref, tab, up)

    return pl.pallas_call(
        kernel,
        out_shape=(
            jax.ShapeDtypeStruct((TOP * BS, BS), jnp.float32),
            jax.ShapeDtypeStruct((BS, BS), jnp.float32),
        ),
        in_specs=[smem()] + [vmem()] * 3,
        out_specs=[vmem(), vmem()],
        scratch_shapes=[pltpu.VMEM(s, jnp.float32) for s in STATE] + factor_scratch(),
        compiler_params=params(),
        cost_estimate=pl.CostEstimate(flops=15 * 10**9, bytes_accessed=4 << 20, transcendentals=0),
        name="cholesky_last",
    )(place, *state)


def assemble_kernel(slot_ref, front_ref, child_ref, out_ref):
    out_ref[...] = front_ref[...]
    for i in range(16):
        slot = slot_ref[i]
        out_ref[slot] = out_ref[slot] + child_ref[:, i, :]


def assemble(slots, front, child):
    return pl.pallas_call(
        assemble_kernel,
        out_shape=jax.ShapeDtypeStruct(front.shape, jnp.float32),
        in_specs=[smem(), vmem(), vmem()],
        out_specs=vmem(),
        compiler_params=params(),
        name="assemble",
    )(slots, front, child)


ORDER = (0, 1, 3, 2)


def split(x):
    big = x.astype(jnp.bfloat16)
    return big, (x - big.astype(jnp.float32)).astype(jnp.bfloat16)


def set_weights(place_ref, weight_ref, high, wide):
    my_z = place_ref[1] % 4
    for at, dz in enumerate(ORDER):
        start = pl.multiple_of((my_z + 4 - dz) % 4 * BS, BS)
        big, small = split(weight_ref[pl.ds(start, BS), :])
        high[at * BS : (at + 1) * BS, :] = big
        wide[at * BS : (at + 1) * BS, :BS] = big
        wide[at * BS : (at + 1) * BS, BS:] = small


def product(parts, high, wide):
    panel = jnp.concatenate([x.reshape(GROUP * SUB, BS) for x in parts], axis=1)
    big, small = split(panel)
    one = lax.dot_general(big, wide, NN, preferred_element_type=jnp.float32)
    two = lax.dot_general(small, high, NN, preferred_element_type=jnp.float32)
    return (one[:, :BS] + (one[:, BS:] + two)).reshape(GROUP, SUB, BS)


def chunk_rows(place_ref, dy):
    return pl.ds(pl.multiple_of((place_ref[1] // 4 + 4 - dy) % 4 * SUB, SUB), SUB)


def near_kernel(steps, place_ref, which_ref, weight_ref, top_ref, child_ref, *refs):
    first, second, (front_ref, out_ref, high, wide) = refs[:6], refs[6:12], refs[12:]
    step = pl.program_id(0)
    mine = place_ref[1] >= TOP

    @pl.when(step == 0)
    def _():
        set_weights(place_ref, weight_ref, high, wide)

    @pl.when(step < steps)
    def _():
        for dy in range(4):
            rows = chunk_rows(place_ref, dy)
            base = jnp.where(mine, front_ref[:, rows, :], 0.0)
            if dy == 2:
                out_ref[:, rows, :] = base
            else:
                at = 2 * ORDER.index(dy)
                parts = [first[at + dz // 2][dz % 2] for dz in ORDER]
                out_ref[:, rows, :] = base - product(parts, high[...], wide[...])

    @pl.when(step >= steps)
    def _():
        for dy in range(4):
            rows = chunk_rows(place_ref, dy)
            base = jnp.where(mine, front_ref[:, rows, :], 0.0)
            parts = [second[2 * at + dy // 2][dy % 2] for at in range(3)]
            out_ref[:, rows, :] = base - product(parts, high[: 3 * BS], wide[: 3 * BS])

    @pl.when(mine)
    def _():
        for i in range(GROUP):
            for c in range(2):
                source = which_ref[c, step * GROUP + i]

                @pl.when(source >= 0)
                def _():
                    out_ref[i] = out_ref[i] + child_ref[jnp.maximum(source, 0)]

    @pl.when((step == 0) & (place_ref[0] < TOP))
    def _():
        out_ref[0] = top_ref[...]


def far_kernel(steps, place_ref, weight_ref, a_low, a_high, b_low, b_high, prev_ref, out_ref, high, wide):
    step = pl.program_id(0)

    @pl.when(step == 0)
    def _():
        set_weights(place_ref, weight_ref, high, wide)

    out_ref[...] = prev_ref[...]

    @pl.when(step < steps)
    def _():
        rows = chunk_rows(place_ref, 2)
        parts = [(a_low, a_high)[dz // 2][dz % 2] for dz in ORDER]
        out_ref[:, rows, :] = prev_ref[:, rows, :] - product(parts, high[...], wide[...])

    @pl.when(step >= steps)
    def _():
        for dy in range(4):
            rows = chunk_rows(place_ref, dy)
            parts = [(b_low, b_high)[dy // 2][dy % 2]]
            out_ref[:, rows, :] = prev_ref[:, rows, :] - product(parts, high[3 * BS :], wide[3 * BS :])

    @pl.when((step == 0) & (place_ref[0] < TOP))
    def _():
        out_ref[0] = prev_ref[0]


def piece_specs(first, second):
    steps = PART // GROUP
    early = lambda i: (0, jnp.minimum(i, steps - 1), 0, 0)
    late = lambda i: (0, jnp.maximum(i - steps, 0), 0, 0)
    specs = [pl.BlockSpec((2, GROUP, SUB, BS), early) for _ in first]
    return specs + [pl.BlockSpec((2, GROUP, SUB, BS), late) for _ in second]


def weight_scratch():
    return [pltpu.VMEM((TOP * BS, BS), jnp.bfloat16), pltpu.VMEM((TOP * BS, 2 * BS), jnp.bfloat16)]


def near_update(place, which, weight, top, child, first, second, front):
    block = pl.BlockSpec((GROUP, BS, BS), lambda i: (i, 0, 0))
    return pl.pallas_call(
        functools.partial(near_kernel, PART // GROUP),
        out_shape=jax.ShapeDtypeStruct(front.shape, jnp.float32),
        grid=(pl.cdiv(front.shape[0], GROUP),),
        in_specs=[smem(), smem(), vmem(), vmem(), vmem()] + piece_specs(first, second) + [block],
        out_specs=block,
        scratch_shapes=weight_scratch(),
        compiler_params=params(),
        cost_estimate=pl.CostEstimate(flops=10**10, bytes_accessed=20 << 20, transcendentals=0),
        name="near_update",
    )(place, which, weight, top, child, *first, *second, front)


def far_update(place, weight, first, second, result):
    block = pl.BlockSpec((GROUP, BS, BS), lambda i: (i, 0, 0))
    return pl.pallas_call(
        functools.partial(far_kernel, PART // GROUP),
        out_shape=jax.ShapeDtypeStruct(result.shape, jnp.float32),
        grid=(pl.cdiv(result.shape[0], GROUP),),
        in_specs=[smem(), vmem()] + piece_specs(first, second) + [block],
        out_specs=block,
        input_output_aliases={6: 0},
        scratch_shapes=weight_scratch(),
        compiler_params=params(),
        cost_estimate=pl.CostEstimate(flops=3 * 10**9, bytes_accessed=12 << 20, transcendentals=0),
        name="far_update",
    )(place, weight, *first, *second, result)


Y_STEP = 4
Z_STEP = 1


def shift(x, axis, by):
    if axis == Y_STEP:
        pairs = [(4 * y + z, 4 * ((y + by) % 4) + z) for y in range(4) for z in range(4)]
    else:
        pairs = [(4 * y + z, 4 * y + (z + by) % 4) for y in range(4) for z in range(4)]
    return lax.ppermute(x, "pcol", pairs)


SAME_Y = [[p * PCOLS + 4 * y + z for z in range(4) for p in range(PROWS)] for y in range(4)]


def hop(x, origin, target):
    return lax.ppermute(x, "pcol", [(4 * origin + z, 4 * target + z) for z in range(4)])


def on_device(front, child, row_map, col_map):
    count = front.shape[0]
    row_here = lax.axis_index("prow")
    col_here = lax.axis_index("pcol")
    place = jnp.stack([row_here, col_here]).astype(jnp.int32)
    blocks = front.reshape(count, BS, BS)
    pieces = child.reshape(16, BS, BS)
    by_source = row_map.reshape(2, 8, PROWS).transpose(0, 2, 1)
    table = by_source.reshape(2, 64)
    mine = by_source % PROWS == row_here
    slots = jnp.sum(jnp.where(mine, by_source // PROWS, 0), axis=2)
    padded = pl.cdiv(count, GROUP) * GROUP
    hit = slots[:, :, None] == jnp.arange(padded)[None, None, :]
    which = jnp.max(jnp.where(hit, jnp.arange(16).reshape(2, 8, 1), -1), axis=1)
    cuts = [blocks[:, y * SUB : (y + 1) * SUB] for y in range(4)]
    half = count // 2
    relay = [hop(cuts[2][:half], 0, 1), hop(cuts[2][half:], 0, 3)]
    sent = [hop(cuts[1], 0, 1), hop(cuts[3], 0, 3)]
    first = jnp.concatenate([pieces, blocks[:2], jnp.zeros((6, BS, BS), jnp.float32)])
    first = first.reshape(24, PCOLS, PROWS, BS).transpose(2, 1, 0, 3).reshape(BS, 24, BS)
    got = lax.all_to_all(first, BOTH, 0, 0, tiled=True)
    got, relay = lax.optimization_barrier((got, relay))
    sent = sent + [hop(relay[0], 1, 2), hop(relay[1], 3, 2)]
    panel, mixed = route(col_map, table, got.reshape(PROWS, PCOLS, 24, BS))
    panel = lax.all_to_all(
        panel.reshape(4 * PROWS, 16, BS), BOTH, 0, 0, tiled=True, axis_index_groups=SAME_Y
    )
    summed = jnp.where(col_here < TOP, cuts[0], sent[0] + sent[1] + jnp.concatenate(sent[2:]))
    chunk = assemble(slots.reshape(16), summed, panel)
    half = PART // 2
    rings = (Y_STEP, Z_STEP)
    around, pairs = [], []
    for part, ring in ((chunk[:PART], Z_STEP), (chunk[PART:], Y_STEP)):
        after, before = shift(part, ring, 1), shift(part, ring, -1)
        around.append((after, before))
        pairs.append(jnp.stack([part, after]))
    mixed, _ = lax.optimization_barrier((mixed, around))
    known = lax.all_to_all(mixed.reshape(BS, WIDE, BS), BOTH, 0, 0, tiled=True)
    near = [[shift(x, r, d) for d in (1, -1)] for x, r in zip(pairs, rings)]
    reach = []
    for (after, before), ring in zip(around, (Z_STEP, Y_STEP)):
        reach.append([shift(after[:half], ring, 1), shift(before[half:], ring, -1)])
    known, _ = lax.optimization_barrier((known, reach))
    state = cholesky_first(known)
    reach, state = lax.optimization_barrier((reach, state))
    ends = [jnp.stack([jnp.concatenate(far), before]) for far, (_, before) in zip(reach, around)]
    rest = [[shift(x, r, d) for d in (1, -1)] for x, r in zip(ends, rings)]
    near, state, _ = lax.optimization_barrier((near, state, ends))
    near_far = [shift(x[0], r, 1) for x, r in zip(near, rings)]
    weight, top = cholesky_last(place, state)
    rest, weight = lax.optimization_barrier((rest, weight))
    rest_far = [shift(x[1], r, -1) for x, r in zip(rest, rings)]
    arrived = known[:, 16:]
    arrived = arrived.reshape(PROWS, PCOLS, 16, BS).transpose(2, 1, 0, 3).reshape(16, BS, BS)
    first, second = [
        [pairs[i], ends[i], near[i][0], rest[i][0], near[i][1], rest[i][1]] for i in range(2)
    ]
    result = near_update(place, which, weight, top, arrived, first, second, blocks)
    first, second = [[near_far[i], rest_far[i]] for i in range(2)]
    result = far_update(place, weight, first, second, result)
    return result.reshape(front.shape)


def solution(mesh):
    return jax.shard_map(
        on_device,
        mesh=mesh,
        in_specs=(
            P(None, "prow", None, None, "pcol", None),
            P(None, None, "prow", None, "pcol", None),
            P(),
            P(),
        ),
        out_specs=P(None, "prow", None, None, "pcol", None),
        check_vma=False,
    )
```
